32 devices in a mesh: dp: 16 (over z, x, core), tensor: 2 (over y).
Axes of the slice: x: 2, y: 2, z: 4, core: 2. Of those that a mesh axis runs over, the one named last changes fastest.
Arguments:
- tokens: bfloat16 [16384, 768], P(('dp', 'tensor')), may hold values from -6 to 6
- w_qkv: bfloat16 [3, 768, 768], P(None, None, 'tensor'), may hold values from -0.21875 to 0.21875
- attn_bias: float32 [2, 768], P(None, 'tensor'), may hold values from -3 to 3
- w_out: bfloat16 [768, 768], P('tensor'), may hold values from -0.875 to 0.875
- res_bias: float32 [2, 768], replicated, may hold values from -3 to 3
- w_in: bfloat16 [768, 3072], P(None, 'tensor'), may hold values from -0.21875 to 0.21875
- ffn_bias: float32 [3072], P('tensor'), may hold values from -3 to 3
- w_back: bfloat16 [3072, 768], P('tensor'), may hold values from -0.109375 to 0.109375
- norm_gains: float32 [2, 768], replicated, may hold values from 0.5 to 1.5
- norm_shifts: float32 [2, 768], replicated, may hold values from -3 to 3
- cotangent: bfloat16 [16384, 768], P(('dp', 'tensor')), may hold values from -6 to 6
- buckets: int32 [16], P('dp'), may hold values from 0 to 2, as said below
- lengths: int32 [16, 32], P('dp'), may hold values from 0 to 128, as said below
Outputs:
- output: bfloat16 [16384, 768], P(('dp', 'tensor'))
- grad_tokens: bfloat16 [16384, 768], P(('dp', 'tensor'))
- grad_qkv: float32 [3, 768, 768], P(None, None, 'tensor')
- grad_attn_bias: float32 [2, 768], P(None, 'tensor')
- grad_out: float32 [768, 768], P('tensor')
- grad_res_bias: float32 [2, 768], replicated
- grad_in: float32 [768, 3072], P(None, 'tensor')
- grad_ffn_bias: float32 [3072], P('tensor')
- grad_back: float32 [3072, 768], P('tensor')
- grad_norm_gains: float32 [2, 768], replicated
- grad_norm_shifts: float32 [2, 768], replicated
The draws below stay inside these ranges and needn't reach their ends.
Inputs may be any that keep to these rules, and one draw needn't show every extreme that they name: `buckets`: every bucket value 0, 1 and 2 occurs in some row. `lengths`: A row of bucket b holds 1024 / (32 * 2**b) sentences; entry s is the length of the sentence that starts at token s * 32 * 2**b of the row, from 1 to 32 * 2**b, and one sentence of each row fills its slot; the later entries are 0.
All inputs are finite; a program needn't handle non-finite values.
Results may differ from the reference program's by a relative error of at most 0.015.
Values may be sent and summed in bfloat16 or wider, within the bound.
No kernel may reach another device: no remote copies, remote signals or barrier semaphores. Data moves between devices by JAX's collectives and lax.ppermute only.
A program may use at most 128 MiB of HBM per device.

```python
import math
import jax
import jax.numpy as jnp
from jax import lax

D = 768
HEADS = 12
HEAD_DIM = 64
FF = 3072
ROW_LEN = 1024
SLOTS = 32
ROWS = 16
TOKENS = 16384


def row_buckets(key):
    bucket_draw = jax.random.randint(jax.random.fold_in(key, 11), (ROWS,), 0, 3)
    chosen_rows = jax.random.permutation(jax.random.fold_in(key, 12), ROWS)
    bucket_draw = bucket_draw.at[chosen_rows[0]].set(2)
    bucket_draw = bucket_draw.at[chosen_rows[1]].set(0)
    bucket_draw = bucket_draw.at[chosen_rows[2]].set(1)
    return bucket_draw.astype(jnp.int32)


def draw_buckets(key, part):
    shared = row_buckets(key)
    return shared


def draw_lengths(key, part):
    bucket_draw = row_buckets(key)
    key = jax.random.fold_in(key, 5)
    slot_width = jnp.where(bucket_draw == 0, 32, jnp.where(bucket_draw == 1, 64, 128)).astype(jnp.int32)
    slot_count = ROW_LEN // slot_width
    slot_index = jnp.arange(SLOTS, dtype=jnp.int32)
    raw_draw = jax.random.randint(key, (ROWS, SLOTS), 0, 1 << 20)
    length = 1 + raw_draw % slot_width[:, None]
    full_slot = jax.random.randint(jax.random.fold_in(key, 7), (ROWS,), 0, 1 << 20) % slot_count
    length = jnp.where(slot_index[None, :] == full_slot[:, None], slot_width[:, None], length)
    length = jnp.where(slot_index[None, :] < slot_count[:, None], length, 0)
    return length.astype(jnp.int32)


def raised(values, own_key, source, target, shards_of, factor):
    owner, partner = [(jnp.arange(values.shape[dim]) // (values.shape[dim] // shards_of)).reshape([-1 if axis == dim else 1 for axis in range(values.ndim)]) for dim in (source, target)]
    chosen = jax.random.permutation(own_key, shards_of)[partner]
    strong = (owner == chosen) | (owner == (partner + shards_of // 2) % shards_of)
    return jnp.where(strong, factor * values, values)


def levels(stream_key, dims, shards, low, top_value):
    factor_of = 1.0
    for dim, shards_of in shards:
        heights = jax.random.uniform(jax.random.fold_in(jax.random.fold_in(stream_key, 6), dim), (shards_of,), jnp.float32, low / len(shards), top_value / len(shards))
        factor_of = factor_of * jnp.repeat(jnp.exp(heights), dims[dim] // shards_of).reshape((-1,) + (1,) * (len(dims) - 1 - dim))
    return factor_of


def gaussian(rng, extent, deviation, bound, pieces=(), kind=jnp.bfloat16):
    factor_of = levels(rng, extent, pieces, -0.22, 0.18) if pieces else 1.0
    values = jax.random.normal(rng, extent, jnp.float32) * deviation * factor_of
    return jnp.minimum(jnp.maximum(values, -bound), bound).astype(kind)


def noise_with(key, extent, scale, reach, shards, heavy, kind=jnp.bfloat16):
    drawn = scale * jax.random.normal(key, extent, jnp.float32)
    if shards:
        drawn = drawn * levels(key, extent, shards, -0.22, 0.18)
    return jnp.clip(raised(drawn, jax.random.fold_in(key, 3), *heavy), -reach, reach).astype(kind)


def setup_inputs(seed: int = 0) -> dict:
    arg_keys = jax.random.split(jax.random.key(seed), 14)
    return {
        "tokens": gaussian(arg_keys[0], (TOKENS, D), 1.0, 6.0, ((0, 32),)),
        "w_qkv": gaussian(arg_keys[1], (3, D, D), D ** -0.5, 0.21875, ((2, 2),)),
        "attn_bias": gaussian(arg_keys[2], (2, D), 0.5, 3.0, ((1, 2),), jnp.float32),
        "w_out": gaussian(arg_keys[3], (D, D), (D // 16) ** -0.5, 0.875, ((0, 2),)),
        "res_bias": gaussian(arg_keys[4], (2, D), 0.5, 3.0, (), jnp.float32),
        "w_in": gaussian(arg_keys[5], (D, FF), D ** -0.5, 0.21875, ((1, 2),)),
        "ffn_bias": gaussian(arg_keys[6], (FF,), 0.5, 3.0, ((0, 2),), jnp.float32),
        "w_back": gaussian(arg_keys[7], (FF, D), FF ** -0.5, 0.109375, ((0, 2),)),
        "norm_gains": jnp.clip(1.0 + 0.1 * jax.random.normal(arg_keys[8], (2, D), jnp.float32), 0.5, 1.5),
        "norm_shifts": gaussian(arg_keys[9], (2, D), 0.5, 3.0, (), jnp.float32),
        "cotangent": noise_with(arg_keys[10], (TOKENS, D), 1.0, 6.0, ((0, 32),), (0, 1, 32, 2.75)),
        "buckets": draw_buckets(jax.random.fold_in(arg_keys[13], 71), 0),
        "lengths": draw_lengths(jax.random.fold_in(arg_keys[13], 71), 0),
    }


@jax.custom_vjp
def low(v):
    return lax.optimization_barrier(v.astype(jnp.bfloat16)).astype(jnp.float32)

@jax.custom_vjp
def low_back(v):
    return v

def low_keep(v):
    return (low(v), None)

def low_pass(kept, grad):
    return (grad,)

def back_keep(v):
    return (v, None)

def back_low(kept, grad):
    return (low(grad),)
low.defvjp(low_keep, low_pass)
low_back.defvjp(back_keep, back_low)
highest = lax.Precision.HIGHEST
neg_fill = -1000000000.0
norm_eps = 1e-05
tile_width = 128
inv_root_two = 1.0 / math.sqrt(2.0)

def both_round(values):
    return low(low_back(values))

def slot_mask(bucket, length_row):
    slot_width = jnp.where(bucket == 0, 32, jnp.where(bucket == 1, 64, 128)).astype(jnp.int32)
    token_place = jnp.arange(ROW_LEN, dtype=jnp.int32)
    slot_id = token_place // slot_width
    inside = token_place - slot_id * slot_width
    slot_match = slot_id[:, None] == jnp.arange(length_row.shape[0], dtype=jnp.int32)[None, :]
    length = lax.optimization_barrier(jnp.sum(jnp.where(slot_match, length_row[None, :], 0), axis=1)).astype(jnp.int32)
    slot_id = slot_id.reshape(-1, tile_width)
    inside = inside.reshape(-1, tile_width)
    length = length.reshape(-1, tile_width)
    same_slot = slot_id[:, :, None] == slot_id[:, None, :]
    return jnp.logical_and(same_slot, inside[:, None, :] < length[:, None, :])

def layer_norm(values, gain_row, shift_row):
    centred = values - lax.optimization_barrier(jnp.mean(values, axis=-1, keepdims=True))
    inv_root = lax.rsqrt(lax.optimization_barrier(jnp.mean(centred * centred, axis=-1, keepdims=True)) + norm_eps)
    return centred * inv_root * gain_row + shift_row

def gelu_value(pre_act):
    return 0.5 * pre_act * (1.0 + lax.erf(pre_act * inv_root_two))

def by_tile(array_in):
    return array_in.reshape(-1, tile_width, HEADS, HEAD_DIM)

def forward(x_row, allowed, w_qkv, attn_bias, w_out, res_bias, w_in, ffn_bias, w_back, norm_gains, norm_shifts):
    queries = both_round(jnp.dot(x_row, w_qkv[0], precision=highest) + attn_bias[0])
    keys_b = both_round(jnp.dot(x_row, w_qkv[1], precision=highest))
    values_b = both_round(jnp.dot(x_row, w_qkv[2], precision=highest) + attn_bias[1])
    raw_scores = jnp.einsum('tqhd,tkhd->thqk', by_tile(queries), by_tile(keys_b), precision=highest) * HEAD_DIM ** (-0.5)
    scores = jnp.where(allowed[:, None], low_back(raw_scores), neg_fill)
    row_top = lax.optimization_barrier(jnp.max(scores, axis=-1, keepdims=True))
    exp_scores = jnp.exp(scores - row_top)
    attn_probs = exp_scores / lax.optimization_barrier(jnp.sum(exp_scores, axis=-1, keepdims=True))
    context = jnp.einsum('thqk,tkhd->tqhd', low(attn_probs), by_tile(values_b), precision=highest)
    context = both_round(context.reshape(ROW_LEN, D))
    attended = low_back(jnp.dot(context, w_out, precision=highest) + res_bias[0])
    normed_mid = layer_norm(x_row + attended, norm_gains[0], norm_shifts[0])
    pre_act = low_back(jnp.dot(low(normed_mid), w_in, precision=highest) + ffn_bias)
    hidden = low(gelu_value(pre_act))
    ffn_out = low_back(jnp.dot(hidden, w_back, precision=highest) + res_bias[1])
    return layer_norm(normed_mid + ffn_out, norm_gains[1], norm_shifts[1])

def reference(tokens, w_qkv, attn_bias, w_out, res_bias, w_in, ffn_bias, w_back, norm_gains, norm_shifts, cotangent, buckets, lengths):
    params = tuple((array_in.astype(jnp.float32) for array_in in (w_qkv, attn_bias, w_out, res_bias, w_in, ffn_bias, w_back, norm_gains, norm_shifts)))
    x_rows = tokens.astype(jnp.float32).reshape(ROWS, ROW_LEN, D)
    g_rows = cotangent.astype(jnp.float32).reshape(ROWS, ROW_LEN, D)

    def row_step(totals, row_item):
        x_row, g_row, bucket, length_row = row_item
        allowed = slot_mask(bucket, length_row)

        def row_forward(x_input, *weights):
            return forward(x_input, allowed, *weights)
        result, pull_back = jax.vjp(row_forward, x_row, *params)
        row_grads = pull_back(g_row)
        totals = tuple((earlier + later for earlier, later in zip(totals, row_grads[1:])))
        return (totals, (result.astype(jnp.bfloat16), row_grads[0].astype(jnp.bfloat16)))
    start_sums = tuple((jnp.zeros_like(array_in) for array_in in params))
    totals, (output, grad_tokens) = lax.scan(row_step, start_sums, (x_rows, g_rows, buckets, lengths))
    return (output.reshape(TOKENS, D), grad_tokens.reshape(TOKENS, D), totals[0], totals[1], totals[2], totals[3], totals[4], totals[5], totals[6], totals[7], totals[8])
```

```python
import math

import jax
import jax.numpy as jnp
from jax import lax
from jax.sharding import PartitionSpec as P

HEAD_DIM = 64
ROW_LEN = 1024


neg_fill = -1000000000.0
norm_eps = 1e-05
tile_width = 128
inv_root_two = 1.0 / math.sqrt(2.0)
inv_root_tau = 1.0 / math.sqrt(2.0 * math.pi)
f32 = jnp.float32
bf16 = jnp.bfloat16


def slot_mask(bucket, length_row):
    slot_width = jnp.where(bucket == 0, 32, jnp.where(bucket == 1, 64, 128)).astype(jnp.int32)
    token_place = jnp.arange(ROW_LEN, dtype=jnp.int32)
    slot_id = token_place // slot_width
    inside = token_place - slot_id * slot_width
    slot_match = slot_id[:, None] == jnp.arange(length_row.shape[0], dtype=jnp.int32)[None, :]
    length = jnp.sum(jnp.where(slot_match, length_row[None, :], 0), axis=1)
    slot_id = slot_id.reshape(-1, tile_width)
    inside = inside.reshape(-1, tile_width)
    length = length.reshape(-1, tile_width)
    same_slot = slot_id[:, :, None] == slot_id[:, None, :]
    return jnp.logical_and(same_slot, inside[:, None, :] < length[:, None, :])


def layer_norm(values, gain_row, shift_row):
    centred = values - jnp.mean(values, axis=-1, keepdims=True)
    inv_root = lax.rsqrt(jnp.mean(centred * centred, axis=-1, keepdims=True) + norm_eps)
    normed = centred * inv_root
    return (normed * gain_row + shift_row, normed, inv_root)


def norm_back(grad_result, normed, inv_root, gain_row):
    grad_normed = grad_result * gain_row
    return inv_root * (
        grad_normed
        - jnp.mean(grad_normed, axis=-1, keepdims=True)
        - normed * jnp.mean(grad_normed * normed, axis=-1, keepdims=True)
    )


def gelu_both(pre_act):
    cdf = 0.5 * (1.0 + lax.erf(pre_act * inv_root_two))
    return pre_act * cdf, cdf + pre_act * jnp.exp(-0.5 * pre_act * pre_act) * inv_root_tau


def per_device(dp_size, *args):
    (tokens, w_qkv, attn_bias, w_out, res_bias, w_in, ffn_bias, w_back,
     norm_gains, norm_shifts, cotangent, buckets, lengths) = args
    here = lax.axis_index("dp")
    side = lax.axis_index("tensor")
    n_bits = dp_size.bit_length() - 1
    assert 1 << n_bits == dp_size and n_bits >= 4

    def bit(b):
        return (here >> b) & 1

    def over_dp(value, b):
        return lax.ppermute(value, "dp", [(i, i ^ (1 << b)) for i in range(dp_size)])

    def over_tensor(value):
        return lax.ppermute(value, "tensor", [(0, 1), (1, 0)])

    def take(value, index, count):
        size = value.shape[0] // count
        return lax.dynamic_slice_in_dim(value, index * size, size, 0)

    def ordered(mine, theirs, b):
        low = jnp.where(b == 0, mine, theirs)
        high = jnp.where(b == 0, theirs, mine)
        return low, high

    def fetch(weight):
        mine = over_tensor(take(weight, (here & 3), 4))
        next_x = over_dp(mine, 1)
        low, high = ordered(mine, next_x, bit(1))
        pair = jnp.stack([low, high])
        other = over_dp(pair, 0)
        low, high = ordered(pair, other, bit(0))
        return jnp.stack([low, high], axis=1).reshape(weight.shape)

    half_width = w_qkv.shape[2]
    half_heads = half_width // HEAD_DIM
    score_scale = HEAD_DIM ** (-0.5)
    n_tokens = tokens.shape[0]
    allowed = jax.vmap(slot_mask)(buckets, lengths).reshape(-1, tile_width, tile_width)
    allowed = take(allowed, side, 2)

    w_qkv_other = fetch(w_qkv.reshape(-1, half_width)).reshape(w_qkv.shape)
    w_out_other = fetch(w_out)
    w_in_other = fetch(w_in)
    w_back_other = fetch(w_back)
    attn_bias_other = over_tensor(attn_bias)
    ffn_bias_other = over_tensor(ffn_bias)
    qkv_w = (w_qkv, w_qkv_other)
    out_w = (w_out, w_out_other)
    in_w = (w_in, w_in_other)
    back_w = (w_back, w_back_other)
    qkv_b = (attn_bias, attn_bias_other)
    in_b = (ffn_bias, ffn_bias_other)

    def by_tile(array_in):
        return array_in.reshape(-1, tile_width, half_heads, HEAD_DIM)

    def attend(weight, bias):
        projected = jnp.einsum("nd,cde->cne", tokens, weight, preferred_element_type=f32)
        queries = (projected[0] + bias[0]).astype(bf16)
        keys = projected[1].astype(bf16)
        values = (projected[2] + bias[1]).astype(bf16)
        raw = jnp.einsum("tqhd,tkhd->thqk", by_tile(queries), by_tile(keys), preferred_element_type=f32)
        scores = jnp.where(allowed[:, None], raw * score_scale, neg_fill)
        exp_scores = jnp.exp(scores - jnp.max(scores, axis=-1, keepdims=True))
        probs = exp_scores / jnp.sum(exp_scores, axis=-1, keepdims=True)
        context = jnp.einsum(
            "thqk,tkhd->tqhd", probs.astype(bf16), by_tile(values), preferred_element_type=f32
        )
        context = context.reshape(n_tokens, half_width).astype(bf16)
        return queries, keys, values, probs, context

    def dot(a, b, dims):
        return lax.dot_general(a, b, (dims, ((), ())), preferred_element_type=f32)

    nn, nt, tn = ((1,), (0,)), ((1,), (1,)), ((0,), (0,))

    kept = [attend(w, b) for w, b in zip(qkv_w, qkv_b)]
    attended = sum(dot(k[4], w, nn) for k, w in zip(kept, out_w)) + res_bias[0]
    mid, normed_one, inv_one = layer_norm(tokens.astype(f32) + attended, norm_gains[0], norm_shifts[0])
    mid_low = mid.astype(bf16)
    hidden, slope = [], []
    for w, b in zip(in_w, in_b):
        value, grad = gelu_both(dot(mid_low, w, nn) + b)
        hidden.append(value.astype(bf16))
        slope.append(grad.astype(bf16))
    ffn_out = sum(dot(h, w, nn) for h, w in zip(hidden, back_w)) + res_bias[1]
    result, normed_two, inv_two = layer_norm(mid + ffn_out, norm_gains[1], norm_shifts[1])
    output = result.astype(bf16)

    def all_sum(own, other):
        shape = own.shape
        half = shape[0] // 2
        own = own.astype(bf16)
        other = other.astype(bf16)
        got = over_dp(jnp.concatenate([take(own, 1 - bit(0), 2), take(other, 1 - bit(0), 2)]), 0)
        away = take(other, bit(0), 2).astype(f32) + got[half:].astype(f32)
        got_y = over_tensor(away.astype(bf16))
        total = take(own, bit(0), 2).astype(f32) + got[:half].astype(f32) + got_y.astype(f32)
        for b in (1, 2, 3):
            away = take(total, 1 - bit(b), 2).astype(bf16)
            total = take(total, bit(b), 2) + over_dp(away, b).astype(f32)
        total = total.astype(bf16)
        for b in range(4, n_bits):
            total = (total.astype(f32) + over_dp(total, b).astype(f32)).astype(bf16)
        for b in (3, 2, 1, 0):
            total = jnp.concatenate(ordered(total, over_dp(total, b), bit(b)))
        return total.reshape(shape)

    def small_sum(value):
        value = value + over_tensor(value)
        for b in range(n_bits):
            value = value + over_dp(value, b)
        return value

    grad_result = cotangent.astype(f32)
    grad_two = norm_back(grad_result, normed_two, inv_two, norm_gains[1])
    grad_fed = grad_two.astype(bf16)
    grad_back = all_sum(*(dot(h, grad_fed, tn) for h in hidden))
    grad_pre = [
        (dot(grad_fed, w, nt) * s.astype(f32)).astype(bf16) for w, s in zip(back_w, slope)
    ]
    grad_in = all_sum(*(dot(mid_low, g, tn) for g in grad_pre))
    grad_ffn_bias = [jnp.sum(g, axis=0, dtype=f32) for g in grad_pre]
    grad_mid = grad_two + sum(dot(g, w, nt) for g, w in zip(grad_pre, in_w))
    grad_one = norm_back(grad_mid, normed_one, inv_one, norm_gains[0])
    grad_att = grad_one.astype(bf16)
    grad_out = all_sum(*(dot(k[4], grad_att, tn) for k in kept))

    def attend_back(saved, w_o):
        queries, keys, values, probs, _ = saved
        grad_context = by_tile(dot(grad_att, w_o, nt).astype(bf16))
        grad_probs = jnp.einsum(
            "tqhd,tkhd->thqk", grad_context, by_tile(values), preferred_element_type=f32
        )
        grad_values = jnp.einsum(
            "thqk,tqhd->tkhd", probs.astype(bf16), grad_context, preferred_element_type=f32
        )
        grad_scores = (
            probs * (grad_probs - jnp.sum(probs * grad_probs, axis=-1, keepdims=True))
        ).astype(bf16)
        grad_queries = score_scale * jnp.einsum(
            "thqk,tkhd->tqhd", grad_scores, by_tile(keys), preferred_element_type=f32
        )
        grad_keys = score_scale * jnp.einsum(
            "thqk,tqhd->tkhd", grad_scores, by_tile(queries), preferred_element_type=f32
        )
        return [
            g.reshape(n_tokens, half_width).astype(bf16)
            for g in (grad_queries, grad_keys, grad_values)
        ]

    grads = [attend_back(k, w) for k, w in zip(kept, out_w)]
    grad_qkv = jnp.stack(
        [all_sum(*(dot(tokens, g[c], tn) for g in grads)) for c in range(3)]
    )
    grad_tokens = (
        grad_one
        + sum(dot(g[c], w[c], nt) for g, w in zip(grads, qkv_w) for c in range(3))
    ).astype(bf16)

    def whole(own, other):
        low, high = ordered(own, other, side)
        return jnp.concatenate([low, high], axis=-1)

    small = jnp.concatenate(
        [
            jnp.sum(grad_att, axis=0, dtype=f32),
            jnp.sum(grad_fed, axis=0, dtype=f32),
            jnp.sum(grad_mid * normed_one, axis=0),
            jnp.sum(grad_result * normed_two, axis=0),
            jnp.sum(grad_mid, axis=0),
            jnp.sum(grad_result, axis=0),
            whole(*grad_ffn_bias),
        ]
    )
    small = small_sum(small)
    late = small_sum(
        jnp.concatenate(
            [whole(*(jnp.sum(g[c], axis=0, dtype=f32) for g in grads)) for c in (0, 2)]
        )
    )
    width = tokens.shape[1]
    pairs = small[: 6 * width].reshape(3, 2, width)
    return (
        output,
        grad_tokens,
        grad_qkv.astype(f32),
        take(late.reshape(2, 2, half_width).swapaxes(0, 1), side, 2)[0],
        grad_out.astype(f32),
        pairs[0],
        grad_in.astype(f32),
        take(small[6 * width :], side, 2),
        grad_back.astype(f32),
        pairs[1],
        pairs[2],
    )


def solution(mesh):
    dp_size = mesh.shape["dp"]
    placed = (
        P(("dp", "tensor"), None),
        P(None, None, "tensor"),
        P(None, "tensor"),
        P("tensor", None),
        P(),
        P(None, "tensor"),
        P("tensor"),
        P("tensor", None),
        P(),
        P(),
        P(("dp", "tensor"), None),
        P("dp"),
        P("dp", None),
    )
    return jax.shard_map(
        lambda *args: per_device(dp_size, *args),
        mesh=mesh,
        in_specs=placed,
        out_specs=(
            P(("dp", "tensor"), None),
            P(("dp", "tensor"), None),
            P(None, None, "tensor"),
            P(None, "tensor"),
            P("tensor", None),
            P(),
            P(None, "tensor"),
            P("tensor"),
            P("tensor", None),
            P(),
            P(),
        ),
        check_vma=False,
    )
```

```python
import functools
import math

import jax
import jax.numpy as jnp
import numpy as np
from jax import lax
from jax.experimental import pallas as pl
from jax.experimental.pallas import tpu as pltpu
from jax.sharding import PartitionSpec as P

HEAD_DIM = 64
ROW_LEN = 1024
TILE = 128
PAIR = 2 * HEAD_DIM
NEG = -1000000000.0
EPS = 1e-05
SCALE = HEAD_DIM ** (-0.5)
inv_root_two = 1.0 / math.sqrt(2.0)
inv_root_tau = 1.0 / math.sqrt(2.0 * math.pi)
f32 = jnp.float32
bf16 = jnp.bfloat16
MB = 1 << 20
LIMIT = 8
WIDE_LIMIT = 14
WIDE = {"feed_own", "feed_other", "back_grad", "in_grad_own", "in_grad_other", "qkv_grad"}
GRID_LIMIT = 16

NN, NT, TN = ((1,), (0,)), ((1,), (1,)), ((0,), (0,))


def dot(a, b, dims=NN):
    return lax.dot_general(a, b, (dims, ((), ())), preferred_element_type=f32)


def sds(shape, dtype=bf16):
    return jax.ShapeDtypeStruct(shape, dtype)


def vmem():
    return pl.BlockSpec(memory_space=pltpu.VMEM)


def smem():
    return pl.BlockSpec(memory_space=pltpu.SMEM)


COST = pl.CostEstimate(flops=3 * 10**10, bytes_accessed=10**15, transcendentals=0)


LITTLE = pl.CostEstimate(flops=1, bytes_accessed=10**15, transcendentals=0)


def call(body, name, me, ins, outs, scratch=(), cost=COST):
    limit = WIDE_LIMIT if name in WIDE else LIMIT
    return pl.pallas_call(
        body,
        name=name,
        out_shape=outs,
        in_specs=[smem()] + [vmem()] * len(ins),
        out_specs=[vmem()] * len(outs),
        scratch_shapes=scratch,
        compiler_params=pltpu.CompilerParams(vmem_limit_bytes=limit * MB),
        cost_estimate=cost,
    )(me, *ins)


def packed(body, name, me, ins, outs):
    return pl.pallas_call(
        body,
        name=name,
        out_shape=outs,
        in_specs=[smem()] + [pl.BlockSpec(memory_space=pltpu.HBM)] * len(ins),
        out_specs=[vmem()] * len(outs),
        scratch_shapes=[pltpu.SemaphoreType.DMA((3,))],
        compiler_params=pltpu.CompilerParams(vmem_limit_bytes=LIMIT * MB),
        cost_estimate=COST,
    )(me, *[pltpu.with_memory_space_constraint(v, pltpu.HBM) for v in ins])


X, C, Z0, Z1, SIDE = range(5)


def rows_at(start, size):
    return pl.ds(pl.multiple_of(start, 16), size)


def head_lanes():
    return lax.broadcasted_iota(jnp.int32, (TILE, PAIR), 1) < HEAD_DIM


def both_heads(block):
    first = head_lanes()
    zero = jnp.zeros_like(block)
    return jnp.concatenate([jnp.where(first, block, zero), jnp.where(first, zero, block)], axis=0)


def side_by_side(stacked):
    return jnp.where(head_lanes(), stacked[:TILE], stacked[TILE:])


def project(x, w, bias, q, k, v):
    q[...] = (dot(x[...], w[0]) + bias[0]).astype(bf16)
    k[...] = dot(x[...], w[1]).astype(bf16)
    v[...] = (dot(x[...], w[2]) + bias[1]).astype(bf16)


def attention(mask, q, k, v, probs, ctx):
    tokens, width = q.shape
    pairs = width // PAIR
    for t in range(tokens // TILE):
        rows = pl.ds(t * TILE, TILE)
        bias = mask[t]
        bias = jnp.concatenate([bias, bias], axis=0)
        for p in range(pairs):
            lanes = pl.ds(p * PAIR, PAIR)
            queries = both_heads(q[rows, lanes] * jnp.asarray(SCALE, bf16))
            scores = dot(queries, k[rows, lanes], NT) + bias
            raised = jnp.exp(scores - jnp.max(scores, axis=-1, keepdims=True))
            prob = (raised / jnp.sum(raised, axis=-1, keepdims=True)).astype(bf16)
            probs[t * pairs + p] = prob
            ctx[rows, lanes] = side_by_side(dot(prob, v[rows, lanes])).astype(bf16)


def attend_own(me, x, w, bias, mask, q, k, v, probs, ctx, x_t):
    x_t[...] = x[...].T
    project(x, w, bias, q, k, v)
    attention(mask, q, k, v, probs, ctx)


def normed(z):
    centred = z - jnp.mean(z, axis=-1, keepdims=True)
    inv = lax.rsqrt(jnp.mean(centred * centred, axis=-1, keepdims=True) + EPS)
    return centred * inv, inv


def norm_back(grad_normed, n, inv):
    return inv * (
        grad_normed
        - jnp.mean(grad_normed, axis=-1, keepdims=True)
        - n * jnp.mean(grad_normed * n, axis=-1, keepdims=True)
    )


def attn_copies(piece, core, w_qkv, w_out, out, sems, first):
    rows = w_qkv.shape[1] // 8
    half = w_qkv.shape[2]
    out_rows = w_out.shape[0] // 8
    mine = w_out.at[rows_at((2 * piece + core) * out_rows, out_rows)]
    pairs = (
        (w_qkv.at[:, rows_at((2 * piece + core) * rows, rows), :], out.at[0:3]),
        (mine.at[:, 0:half], out.at[3, 0:out_rows]),
        (mine.at[:, half : 2 * half], out.at[3, out_rows : 2 * out_rows]),
    )
    return [pltpu.make_async_copy(a, b, sems.at[first + i]) for i, (a, b) in enumerate(pairs)]


def feed_copies(piece, core, w_in, w_back, out, sems, first):
    model, hidden = w_in.shape
    width, rows = hidden // 4, model // 2
    half = width // 2
    mine = w_back.at[rows_at(piece * width + core * half, half)]
    pairs = (
        (w_in.at[rows_at(core * rows, rows), pl.ds(pl.multiple_of(piece * width, 128), width)], out.at[0:rows]),
        (mine.at[:, 0:width], out.at[rows : rows + half]),
        (mine.at[:, width : 2 * width], out.at[rows + half : rows + 2 * half]),
    )
    return [pltpu.make_async_copy(a, b, sems.at[first + i]) for i, (a, b) in enumerate(pairs)]


def run_copies(copies):
    for copy in copies:
        copy.start()
    for copy in copies:
        copy.wait()


def pack_attn(opposite, me, w_qkv, w_out, out, sems):
    piece = 2 * me[X] + me[Z0]
    run_copies(attn_copies(3 - piece if opposite else piece, me[C], w_qkv, w_out, out, sems, 0))


def pack_feed(opposite, me, w_in, w_back, out, sems):
    piece = 2 * me[X] + me[Z0]
    run_copies(feed_copies(3 - piece if opposite else piece, me[C], w_in, w_back, out, sems, 0))


def pack_biases(me, attn_bias, ffn_bias, biases):
    width = biases.shape[2]
    for i in range(2):
        biases[i] = attn_bias[i : i + 1]
    for i in range(4):
        biases[2 + i] = ffn_bias[pl.ds(i * width, width)].reshape(1, width)


def attend_other(
    me, x, n0, n1_, n2, n3, c0, c1, c2, c3, bias, mask, ctx_own, wo_own, res_bias, gains, shifts,
    q, k, v, probs, ctx, w, wo_all, mid, mid_low, n1, r1,
):
    core = me[C]
    rows = n0.shape[1]
    half = wo_all.shape[1] // 2
    part = rows // 2
    for r, (near, across) in enumerate(((n0, c0), (n1_, c1), (n2, c2), (n3, c3))):
        piece = (2 * me[X] + me[Z0]) ^ r
        for c, block in ((core, near), (1 - core, across)):
            w[:, rows_at((2 * piece + c) * rows, rows), :] = block[0:3]
            wo_all[rows_at((2 * piece + c) * part, part), 0:half] = block[3, 0:part]
            wo_all[rows_at((2 * piece + c) * part, part), half : 2 * half] = block[3, part : 2 * part]
    project(x, w, bias, q, k, v)
    attention(mask, q, k, v, probs, ctx)
    attended = dot(ctx_own[...], wo_own[...]) + dot(ctx[...], wo_all[...]) + res_bias[0:1]
    n_one, inv = normed(x[...].astype(f32) + attended)
    n1[...] = n_one
    r1[...] = inv
    value = n_one * gains[0:1] + shifts[0:1]
    mid[...] = value
    mid_low[...] = value.astype(bf16)


def gelu_both(a):
    cdf = 0.5 * (1.0 + lax.erf(a * inv_root_two))
    return a * cdf, cdf + a * jnp.exp(-0.5 * a * a) * inv_root_tau


def feed_own(me, mid_low, w_in, bias, w_back, hidden, slope, total, mid_t):
    row = jnp.concatenate([bias[2 + i] for i in range(4)], axis=1)
    value, grad = gelu_both(dot(mid_low[...], w_in[...]) + row)
    value = value.astype(bf16)
    hidden[...] = value
    slope[...] = grad.astype(bf16)
    total[...] = dot(value, w_back[...])
    mid_t[...] = mid_low[...].T


def feed_other(
    me, mid_low, bias, f0, f1, f2, f3, c0, c1, c2, c3, total, mid, cotangent, res_bias, gains, shifts,
    hidden, slope, w_in, w_back, output, grad_two, fed, sums,
):
    core = me[C]
    model = w_in.shape[0]
    width = w_in.shape[1] // 4
    rows, half = model // 2, width // 2
    for r, (near, across) in enumerate(((f0, c0), (f1, c1), (f2, c2), (f3, c3))):
        for c, block in ((core, near), (1 - core, across)):
            w_in[rows_at(c * rows, rows), r * width : (r + 1) * width] = block[0:rows]
            to = rows_at(r * width + c * half, half)
            w_back[to, 0:width] = block[rows : rows + half]
            w_back[to, width : 2 * width] = block[rows + half : rows + 2 * half]
    row = jnp.concatenate([bias[2 + ((2 * me[X] + me[Z0]) ^ r)] for r in range(4)], axis=1)
    value, grad = gelu_both(dot(mid_low[...], w_in[...]) + row)
    value = value.astype(bf16)
    hidden[...] = value
    slope[...] = grad.astype(bf16)
    ffn = total[...] + res_bias[1:2] + dot(value, w_back[...])
    n2, inv = normed(mid[...] + ffn)
    output[...] = (n2 * gains[1:2] + shifts[1:2]).astype(bf16)
    g = cotangent[...].astype(f32)
    grad = norm_back(g * gains[1:2], n2, inv)
    grad_two[...] = grad
    low = grad.astype(bf16)
    fed[...] = low
    sums[0:1] = jnp.sum(low.astype(f32), axis=0, keepdims=True)
    sums[1:2] = jnp.sum(g * n2, axis=0, keepdims=True)
    sums[2:3] = jnp.sum(g, axis=0, keepdims=True)


def slot(core, own_or_other, rx, r0):
    first = core == 0
    return jnp.where(first, own_or_other, r0), jnp.where(first, rx, own_or_other), jnp.where(first, r0, rx)


def relative(me, h, quarter):
    if h:
        return quarter // 2, quarter % 2
    return me[X] ^ (quarter // 2), me[Z0] ^ (quarter % 2)


def back_grad(me, hid_own, hid_other, fed, away, keep, grads):
    core = me[C]
    width = hid_own.shape[1] // 4
    size = width // 4
    for h, hid in enumerate((hid_own, hid_other)):
        grads[h] = dot(hid[...], fed[...], TN).astype(bf16)
        for q in range(4):
            rx, r0 = relative(me, h, q)
            for c, out in ((1 - core, away), (core, keep)):
                for j in range(2):
                    out[*slot(c, h, rx, r0), j] = grads[h, rows_at(q * width + (2 * c + j) * size, size), :]


def in_grad(mid_t, fed, w_back, slope, w_in, bias_sums, place):
    pre = (dot(fed[...], w_back[...], NT) * slope[...].astype(f32)).astype(bf16)
    width = pre.shape[1] // 4
    sums = jnp.sum(pre.astype(f32), axis=0, keepdims=True)
    for q in range(4):
        bias_sums[place(q)] = sums[:, q * width : (q + 1) * width]
    return dot(mid_t[...], pre).astype(bf16), dot(pre, w_in[...], NT)


def in_grad_own(me, mid_t, fed, w_back, slope, w_in, grads, bias_sums, total):
    grads[...], total[...] = in_grad(mid_t, fed, w_back, slope, w_in, bias_sums, lambda q: q)


def in_grad_other(
    me, mid_t, fed, w_back, slope, w_in, grads_own, total_own, grad_two, n1, r1, gains,
    away, keep, bias_sums, grad_one, grad_att, sums, grads,
):
    core, here = me[C], 2 * me[X] + me[Z0]
    grads[...], part = in_grad(mid_t, fed, w_back, slope, w_in, bias_sums, lambda q: here ^ q)
    width = w_in.shape[1] // 4
    size = w_in.shape[0] // 4
    for h, source in ((0, grads_own), (1, grads)):
        for q in range(4):
            rx, r0 = relative(me, h, q)
            for c, out in ((1 - core, away), (core, keep)):
                for j in range(2):
                    out[*slot(c, h, rx, r0), j] = source[
                        rows_at((2 * c + j) * size, size), q * width : (q + 1) * width
                    ]
    grad_mid = grad_two[...] + total_own[...] + part
    n = n1[...]
    sums[1:2] = jnp.sum(grad_mid * n, axis=0, keepdims=True)
    sums[2:3] = jnp.sum(grad_mid, axis=0, keepdims=True)
    grad = norm_back(grad_mid * gains[0:1], n, r1[...])
    grad_one[...] = grad
    low = grad.astype(bf16)
    grad_att[...] = low
    sums[0:1] = jnp.sum(low.astype(f32), axis=0, keepdims=True)


def attend_back(me, grad_att, w_out, ctx, q, k, v, probs, grads, grad_out, gctx):
    half = grad_out.shape[2]
    gctx[...] = dot(grad_att[...], w_out[...], NT).astype(bf16)
    grad = dot(ctx[...], grad_att[...], TN).astype(bf16)
    grad_out[0] = grad[:, :half]
    grad_out[1] = grad[:, half:]
    tokens, width = q.shape
    pairs = width // PAIR
    for t in range(tokens // TILE):
        rows = pl.ds(t * TILE, TILE)
        for p in range(pairs):
            lanes = pl.ds(p * PAIR, PAIR)
            prob = probs[t * pairs + p]
            context = both_heads(gctx[rows, lanes])
            grads[rows, pl.ds(2 * width + p * PAIR, PAIR)] = dot(prob, context, TN).astype(bf16)
            grad_prob = dot(context, v[rows, lanes], NT)
            prob = prob.astype(f32)
            mean = jnp.sum(prob * grad_prob, axis=-1, keepdims=True)
            score = (prob * (grad_prob - mean)).astype(bf16)
            grads[rows, lanes] = (side_by_side(dot(score, k[rows, lanes])) * SCALE).astype(bf16)
            queries = both_heads(q[rows, lanes])
            grads[rows, pl.ds(width + p * PAIR, PAIR)] = (dot(score, queries, TN) * SCALE).astype(bf16)


def qkv_grad(
    me, x_t, own, own_out, oth, oth_out, sums_one, sums_two, ffn_own, ffn_other, away, keep, grads, small,
):
    mx, mc, m0 = me[X], me[C], me[Z0]
    half = keep.shape[5]
    size = half // 8
    small[...] = jnp.zeros_like(small)
    for h, g, out, ffn in ((0, own, own_out, ffn_own), (1, oth, oth_out, ffn_other)):
        grads[h] = dot(x_t[...], g[...]).astype(bf16)
        rows = [s[i : i + 1, j * half : (j + 1) * half] for s in (sums_one, sums_two) for i in range(3) for j in range(2)]
        rows += [ffn[i] for i in range(4)]
        rows += [
            jnp.sum(g[:, c * half : (c + 1) * half].astype(f32), axis=0, keepdims=True) for c in (0, 2)
        ]
        for i, row in enumerate(rows):
            small[h, i // 2, i % 2 : i % 2 + 1] = row
        for core, piece in ((1 - mc, away), (mc, keep)):
            for rx in range(2):
                for r0 in range(2):
                    place = 4 * core + 2 * (mx ^ rx) + (m0 ^ r0)
                    for j in range(2):
                        to = (*slot(core, h, rx, r0), j)
                        for c in range(3):
                            piece[*to, c * size : (c + 1) * size, :] = grads[
                                h, rows_at(size * (2 * place + j), size), c * half : (c + 1) * half
                            ]
                        piece[*to, 3 * size : 4 * size, :] = out[j, rows_at(size * place, size), :]
                        piece[*to, 4 * size : 4 * size + 16, :] = split(small[h, 2 * place + j])


def split(values):
    high = values.astype(bf16).astype(f32)
    rest = values - high
    middle = rest.astype(bf16).astype(f32)
    fill = jnp.zeros((10, values.shape[1]), f32)
    return jnp.concatenate([high, middle, rest - middle, fill], axis=0).astype(bf16)


def joined(rows):
    rows = rows.astype(f32)
    return rows[0:2] + rows[2:4] + rows[4:6]


def token_grad(me, grad_one, own, oth, w_own, w_other, out):
    total = grad_one[...]
    half = w_own.shape[2]
    for g, w in ((own, w_own), (oth, w_other)):
        for c in range(3):
            total += dot(g[:, c * half : (c + 1) * half], w[c], NT)
    out[...] = total.astype(bf16)


def place_rows(me, b0, b1, b2, b3, out):
    place = pl.program_id(0)
    size = b0.shape[2]
    rx, r0 = me[X] ^ (place // 2), me[Z0] ^ (place % 2)
    for c, blocks in ((0, (b0, b2)), (1, (b1, b3))):
        core = me[C] ^ c
        for last, block in enumerate(blocks):

            @pl.when(jnp.where(core == 0, rx, r0) == last)
            def _():
                for j in range(2):
                    start = pl.multiple_of((2 * core + j) * size, 8)
                    out[pl.ds(start, size), :] = block[jnp.where(core == 0, r0, rx), j].astype(f32)


def place_attn(
    me, b0, b1, b2, b3, qkv, w_out, attn_bias, res_bias, ffn_bias, gains, shifts, small,
):
    n = pl.program_id(0)
    half = b0.shape[3]
    size = half // 8
    for c, blocks in ((0, (b0, b2)), (1, (b1, b3))):
        core = me[C] ^ c
        for last, block in enumerate(blocks):
            for inner in range(2):
                rx, r0 = jnp.where(core == 0, last, inner), jnp.where(core == 0, inner, last)
                start = 4 * core + 2 * (me[X] ^ rx) + (me[Z0] ^ r0)

                @pl.when(n < 3)
                def _():
                    for j in range(2):
                        rows = pl.ds(pl.multiple_of((2 * start + j) * size, 8), size)
                        qkv[0, rows, :] = block[inner, j, rows_at(n * size, size), :].astype(f32)

                @pl.when(n == 3)
                def _():
                    for j in range(2):
                        rows = pl.ds(pl.multiple_of(start * size, 8), size)
                        w_out[rows, j * half : (j + 1) * half] = block[inner, j, 3 * size : 4 * size].astype(f32)
                        small[2 * start + j] = joined(block[inner, j, 4 * size : 4 * size + 16])

    @pl.when(n == 3)
    def _():
        row = lambda i: small[i // 2, i % 2 : i % 2 + 1]
        for out, first in ((res_bias, 0), (gains, 2), (shifts, 4)):
            for i in range(2):
                for j in range(2):
                    out[i : i + 1, j * half : (j + 1) * half] = row(first + 6 * i + j)
        for i in range(4):
            ffn_bias[pl.ds(i * half, half)] = row(12 + i).reshape(half)
        for i in range(2):
            attn_bias[i : i + 1] = row(16 + i)


def add_parts(places, small, me, *refs):
    *ins, out = refs
    lead = out.shape[:-2]
    for i in range(math.prod(lead)):
        at = tuple(int(v) for v in np.unravel_index(i, lead))
        total = ins[0][(*places[0], *at)].astype(f32)
        for place, part in zip(places[1:], ins[1:]):
            total += part[(*place, *at)].astype(f32)
        if small:
            n = out.shape[-2] - 16
            tails = [part[(*place, *at)][n:] for place, part in zip(places, ins)]
            out[(*at, slice(0, n))] = total[:n].astype(out.dtype)
            out[(*at, slice(n, n + 16))] = split(sum(joined(t) for t in tails))
        else:
            out[at] = total.astype(out.dtype)


def join(me, a, b, out):
    out[0] = a[...]
    out[1] = b[...]


def tick(me, x, out):
    out[...] = x[...]


def mask_bias(bucket, length_row, side, count):
    width = jnp.where(bucket == 0, 32, jnp.where(bucket == 1, 64, 128)).astype(jnp.int32)
    place = side * count + jnp.arange(count, dtype=jnp.int32)
    slot = place // width
    inside = place - slot * width
    match = slot[:, None] == jnp.arange(length_row.shape[0], dtype=jnp.int32)[None, :]
    length = jnp.sum(jnp.where(match, length_row[None, :], 0), axis=1)
    slot, key_ok = slot.reshape(-1, TILE), (inside < length).reshape(-1, TILE)
    same = slot[:, :, None] == slot[:, None, :]
    return jnp.where(same & key_ok[:, None, :], 0.0, NEG).astype(f32)


ORDER = (
    "back", "in1", "B_S0", "in2", "ab1", "I_S0", "ab2", "qkv+B_p0", "B_S1", "A_S0", "I_S1", "B_S2",
    "tok", "B_S3", "I_S2", "A_S1", "B_A0", "A_S2", "I_S3", "A_S3+B_g0", "B_A1", "I_A0", "A_A0+B_gc",
    "I_A1", "A_A1", "B_P+I_gc", "I_P+A_gc", "A_P",
)
def per_device(
    dp_size, tokens, w_qkv, attn_bias, w_out, res_bias, w_in, ffn_bias, w_back,
    norm_gains, norm_shifts, cotangent, buckets, lengths,
):
    here = lax.axis_index("dp")
    side = lax.axis_index("tensor")
    n_bits = dp_size.bit_length() - 1
    assert 1 << n_bits == dp_size and n_bits >= 4

    def bit(b):
        return (here >> b) & 1

    me = jnp.stack([bit(1), bit(0), bit(2), bit(3), side]).astype(jnp.int32)

    def over_dp(value, b):
        return lax.ppermute(value, "dp", [(i, i ^ (1 << b)) for i in range(dp_size)])

    def over_tensor(value):
        return lax.ppermute(value, "tensor", [(0, 1), (1, 0)])

    n_tokens, model = tokens.shape
    half = w_qkv.shape[2]
    hidden_half = w_in.shape[1]
    quarter = hidden_half // 4
    n_units = n_tokens // TILE * (half // PAIR)

    def after(value, *others):
        return lax.optimization_barrier((value, *others))[0]

    clock = [me]
    waits = []

    def step(body, *inputs, wait=()):
        flat, tree = jax.tree.flatten(inputs)
        held = lax.optimization_barrier((*flat, clock[0], *jax.tree.leaves(wait), *waits))
        waits.clear()
        out = body(*jax.tree.unflatten(tree, held[: len(flat)]))
        clock[0] = jax.tree.leaves(out)[0]
        return out

    def kernel(body, name, ins, outs, scratch=(), wait=(), cost=COST):
        return step(lambda *a: call(body, name, me, a, outs, scratch=scratch, cost=cost), *ins, wait=wait)

    near_shape = sds((4, model // 8, half))
    feed_shape = sds((model, quarter))
    near, = packed(functools.partial(pack_attn, False), "pack_near", me, (w_qkv, w_out), [near_shape])
    near_y = over_tensor(near)
    clock[0] = near
    biases, = kernel(pack_biases, "pack_biases", (attn_bias, ffn_bias), [sds((6, 1, quarter), f32)])
    biases_other = over_tensor(biases)

    def pack(body, name, opposite, weights, shape, wait=()):
        out, = step(
            lambda *w: packed(functools.partial(body, opposite), name, me, w, [shape]), *weights, wait=wait
        )
        return over_tensor(out)

    feed_y = pack(pack_feed, "pack_feed", False, (w_in, w_back), feed_shape)
    near_d_y = pack(pack_attn, "pack_near_d", True, (w_qkv, w_out), near_shape)
    near_z, near_x = over_dp(near_y, 2), over_dp(near_y, 1)
    feed_d_y = pack(pack_feed, "pack_feed_d", True, (w_in, w_back), feed_shape, wait=(near_y, biases_other))
    mask = step(lambda b, l: mask_bias(b, l, side, n_tokens), buckets[0], lengths[0])

    act = sds((n_tokens, half))
    probs = sds((n_units, 2 * TILE, TILE))
    wide = sds((n_tokens, model), f32)
    column = sds((n_tokens, 1), f32)
    own_q, own_k, own_v, own_p, own_ctx, tokens_t = kernel(
        attend_own, "attend_own", (tokens, w_qkv, biases, mask),
        [act, act, act, probs, act, sds((model, n_tokens))], cost=LITTLE,
    )
    near_c = [over_dp(after(v, own_ctx), 0) for v in (near_y, near_z, near_x)]
    feed_z, feed_x = over_dp(feed_y, 2), over_dp(feed_y, 1)
    turn, = kernel(tick, "tick", (mask[0, :8],), [sds((8, TILE), f32)], wait=(feed_y, *near_c))
    near_all = near_y, near_z, near_x, near_d_y
    near_c.append(over_dp(after(near_d_y, turn), 0))
    (oth_q, oth_k, oth_v, oth_p, oth_ctx, w_qkv_other, w_out_other, mid, mid_low, n1, r1) = kernel(
        attend_other, "attend_other",
        (tokens, *near_all, *near_c, biases_other, mask, own_ctx, w_out,
         res_bias, norm_gains, norm_shifts),
        [act, act, act, probs, act, sds(w_qkv.shape), sds(w_out.shape), wide, sds(tokens.shape), wide, column],
        cost=LITTLE,
    )

    def block(shape, index):
        return pl.BlockSpec(shape, index)

    hidden_own, slope_own, total_own, mid_t = kernel(
        feed_own, "feed_own", (mid_low, w_in, biases, w_back),
        [sds((n_tokens, hidden_half)), sds((n_tokens, hidden_half)), wide, sds((model, n_tokens))],
        wait=feed_y, cost=LITTLE,
    )
    feed_all = feed_y, feed_z, feed_x, feed_d_y
    feed_c = [over_dp(after(v, total_own), 0) for v in feed_all]
    (hidden_other, slope_other, w_in_other, w_back_other, output, grad_two, fed, sums_two) = kernel(
        feed_other, "feed_other",
        (mid_low, biases_other, *feed_all, *feed_c, total_own, mid, cotangent,
         res_bias, norm_gains, norm_shifts),
        [sds((n_tokens, hidden_half)), sds((n_tokens, hidden_half)), sds(w_in.shape),
         sds(w_back.shape), sds(tokens.shape), wide, sds(tokens.shape), sds((3, model), f32)],
    )

    env = {}
    ops = {}
    flying = {}

    def sent(key, value):
        flying[key] = value
        return value

    y, x, z0, z1 = 1, 4, 8, 16
    reduce_steps = (y, z0), (x, y), (z0, x)
    gather_steps = (z0, x), (x, z0)

    def flip(value, partners):
        pairs = [(i, i ^ partners[(i >> 1) & 1]) for i in range(2 * dp_size)]
        return lax.ppermute(value, ("dp", "tensor"), pairs)

    def chain(name, finish):
        state = {}

        def add(name_of, parts, places, shape):
            body = functools.partial(add_parts, places, name == "A")
            return kernel(body, name_of, parts, [sds(shape)])[0]

        def reduce(i):
            def run():
                if i == 0:
                    state["parts"], state["places"] = list(env[name]), [(), ()]
                parts, places = state["parts"], state["places"]
                value = add("add_half", parts, [(*p, 1) for p in places], parts[0].shape[i + 1 :])
                parts.append(sent(f"{name}_p{i}", flip(value, reduce_steps[i])))
                state["places"] = [(*p, 0) for p in places] + [()]

            return run

        def exchange():
            value = add("add_all", state["parts"], state["places"], state["parts"][-1].shape)
            state["pair"] = value, sent(name + "_p3", flip(value, (z1, z1)))

        def gather(i):
            def run():
                pair = state["pair"]
                if i == 0:
                    value = add("add_two", pair, [(), ()], pair[0].shape)
                    for b in range(4, n_bits):
                        value = add("add_two", (value, over_dp(value, b)), [(), ()], value.shape)
                else:
                    value, = kernel(join, "join", pair, [sds((2, *pair[0].shape))])
                got = sent(f"{name}_g{i}", flip(value, gather_steps[i]))
                state["pair"] = value, got
                if i == 1:
                    value_c = sent(name + "_gc", over_dp(value, 0))
                    state["blocks"] = (value, value_c, got, sent(name + "_gc2", over_dp(got, 0)))

            return run

        for i in range(3):
            ops[f"{name}_S{i}"] = reduce(i)
        ops[name + "_S3"] = exchange
        for i in range(2):
            ops[f"{name}_A{i}"] = gather(i)
        ops[name + "_P"] = lambda: env.update({name + "_result": finish(state["blocks"])})

    sub = quarter // 4
    piece = sds((2, 2, 2, 2, sub, model))
    in_piece = sds((2, 2, 2, 2, model // 4, quarter))
    attn_piece = sds((2, 2, 2, 2, half // 2 + 16, half))
    raw_out = sds((2, half, model // 2))

    def back():
        away, keep = kernel(
            back_grad, "back_grad", (hidden_own, hidden_other, fed), [piece, piece],
            scratch=[pltpu.VMEM((2, hidden_half, model), bf16)],
        )
        env["B"] = keep, sent("B_c", over_dp(away, 0))

    def in_first():
        env["in_own"] = kernel(
            in_grad_own, "in_grad_own", (mid_t, fed, w_back, slope_own, w_in),
            [sds(w_in.shape), sds((4, 1, quarter), f32), wide],
        )

    def in_second():
        grads_own, bias_own, mid_own = env["in_own"]
        away, keep, bias_other, grad_one, grad_att, sums_one = kernel(
            in_grad_other, "in_grad_other",
            (mid_t, fed, w_back_other, slope_other, w_in_other, grads_own, mid_own, grad_two, n1, r1, norm_gains),
            [in_piece, in_piece, sds((4, 1, quarter), f32), wide, sds(tokens.shape), sds((3, model), f32)],
            scratch=[pltpu.VMEM(w_in.shape, bf16)],
        )
        env["I"] = keep, sent("I_c", over_dp(away, 0))
        env.update(bias_own=bias_own, bias_other=bias_other, grad_one=grad_one, grad_att=grad_att, sums_one=sums_one)

    def attn_back(w, ctx, q, k, v, p):
        return kernel(
            attend_back, "attend_back", (env["grad_att"], w, ctx, q, k, v, p),
            [sds((n_tokens, 3 * half)), raw_out],
            scratch=[pltpu.VMEM((n_tokens, half), bf16)],
        )

    def attn_first():
        env["own"] = attn_back(w_out, own_ctx, own_q, own_k, own_v, own_p)

    def attn_second():
        env["other"] = attn_back(w_out_other, oth_ctx, oth_q, oth_k, oth_v, oth_p)

    def qkv():
        away, keep = kernel(
            qkv_grad, "qkv_grad",
            (tokens_t, *env["own"], *env["other"], env["sums_one"], sums_two, env["bias_own"], env["bias_other"]),
            [attn_piece, attn_piece],
            scratch=[pltpu.VMEM((2, model, 3 * half), bf16), pltpu.VMEM((2, 16, 2, half), f32)],
        )
        env["A"] = keep, sent("A_c", over_dp(away, 0))

    def token():
        env["grad_tokens"], = kernel(
            token_grad, "token_grad", (env["grad_one"], env["own"][0], env["other"][0], w_qkv, w_qkv_other), [sds(tokens.shape)]
        )

    def placed(body, name, blocks, shapes, outs, scratch=()):
        full = [block(b.shape, lambda s, me, n=b.ndim: (0,) * n) for b in blocks]
        return step(
            lambda *a: pl.pallas_call(
                body,
                name=name,
                grid_spec=pltpu.PrefetchScalarGridSpec(
                    num_scalar_prefetch=1, grid=(4,), in_specs=full, out_specs=outs, scratch_shapes=scratch
                ),
                out_shape=[sds(shape, f32) for shape in shapes],
                compiler_params=pltpu.CompilerParams(vmem_limit_bytes=GRID_LIMIT * MB), cost_estimate=COST,
            )(me, *a),
            *blocks,
        )

    chain("B", lambda blocks: placed(
        place_rows, "place_back", blocks, [w_back.shape], [block((quarter, model), lambda s, me: (s, 0))]
    ))
    chain("I", lambda blocks: placed(
        place_rows, "place_in", blocks, [w_in.shape], [block((model, quarter), lambda s, me: (0, s))]
    ))
    last_shapes = [w_qkv.shape, w_out.shape, (2, half), (2, model), (hidden_half,), (2, model), (2, model)]
    chain("A", lambda blocks: placed(
        place_attn, "place_attn", blocks, last_shapes,
        [block((1, model, half), lambda s, me: (jnp.minimum(s, 2), 0, 0))]
        + [block(shape, lambda s, me, n=len(shape): (0,) * n) for shape in last_shapes[1:]],
        [pltpu.VMEM((16, 2, half), f32)],
    ))
    ops.update({
        "back": back, "in1": in_first, "in2": in_second, "ab1": attn_first, "ab2": attn_second,
        "qkv": qkv, "tok": token,
    })
    for entry in ORDER:
        key, *ended = entry.split("+")
        waits.extend(flying.pop(p) for p in ended)
        ops.pop(key)()
    assert not ops
    grad_tokens = env["grad_tokens"]
    (grad_back,), (grad_in,) = env["B_result"], env["I_result"]
    grad_qkv, grad_out, grad_attn_bias, grad_res_bias, grad_ffn_bias, grad_gains, grad_shifts = env["A_result"]

    return (
        output,
        grad_tokens,
        grad_qkv,
        grad_attn_bias,
        grad_out,
        grad_res_bias,
        grad_in,
        grad_ffn_bias,
        grad_back,
        grad_gains,
        grad_shifts,
    )


def solution(mesh):
    dp_size = mesh.shape["dp"]
    placed = (
        P(("dp", "tensor"), None),
        P(None, None, "tensor"),
        P(None, "tensor"),
        P("tensor", None),
        P(),
        P(None, "tensor"),
        P("tensor"),
        P("tensor", None),
        P(),
        P(),
        P(("dp", "tensor"), None),
        P("dp"),
        P("dp", None),
    )
    return jax.shard_map(
        lambda *args: per_device(dp_size, *args),
        mesh=mesh,
        in_specs=placed,
        out_specs=(
            P(("dp", "tensor"), None),
            P(("dp", "tensor"), None),
            P(None, None, "tensor"),
            P(None, "tensor"),
            P("tensor", None),
            P(),
            P(None, "tensor"),
            P("tensor"),
            P("tensor", None),
            P(),
            P(),
        ),
        check_vma=False,
    )
```

```python
import functools
import math

import jax
import jax.numpy as jnp
import numpy as np
from jax import lax
from jax.experimental import pallas as pl
from jax.experimental.pallas import tpu as pltpu
from jax.sharding import PartitionSpec as P

HEAD_DIM = 64
ROW_LEN = 1024
TILE = 128
PAIR = 2 * HEAD_DIM
NEG = -1000000000.0
EPS = 1e-05
SCALE = HEAD_DIM ** (-0.5)
inv_root_two = 1.0 / math.sqrt(2.0)
inv_root_tau = 1.0 / math.sqrt(2.0 * math.pi)
f32 = jnp.float32
bf16 = jnp.bfloat16
MB = 1 << 20
LIMIT = 8
WIDE_LIMIT = 14
WIDE = {"feed_own", "feed_other", "back_grad", "in_grad_own", "in_grad_other", "qkv_grad"}

NN, NT, TN = ((1,), (0,)), ((1,), (1,)), ((0,), (0,))


def dot(a, b, dims=NN):
    return lax.dot_general(a, b, (dims, ((), ())), preferred_element_type=f32)


def sds(shape, dtype=bf16):
    return jax.ShapeDtypeStruct(shape, dtype)


def vmem():
    return pl.BlockSpec(memory_space=pltpu.VMEM)


def smem():
    return pl.BlockSpec(memory_space=pltpu.SMEM)


COST = pl.CostEstimate(flops=3 * 10**10, bytes_accessed=10**15, transcendentals=0)


LITTLE = pl.CostEstimate(flops=1, bytes_accessed=10**15, transcendentals=0)


def call(body, name, me, ins, outs, scratch=(), cost=COST):
    limit = WIDE_LIMIT if name in WIDE else LIMIT
    return pl.pallas_call(
        body,
        name=name,
        out_shape=outs,
        in_specs=[smem()] + [vmem()] * len(ins),
        out_specs=[vmem()] * len(outs),
        scratch_shapes=scratch,
        compiler_params=pltpu.CompilerParams(vmem_limit_bytes=limit * MB),
        cost_estimate=cost,
    )(me, *ins)


def packed(body, name, me, ins, outs):
    return pl.pallas_call(
        body,
        name=name,
        out_shape=outs,
        in_specs=[smem()] + [pl.BlockSpec(memory_space=pltpu.HBM)] * len(ins),
        out_specs=[vmem()] * len(outs),
        scratch_shapes=[pltpu.SemaphoreType.DMA((3,))],
        compiler_params=pltpu.CompilerParams(vmem_limit_bytes=LIMIT * MB),
        cost_estimate=COST,
    )(me, *[pltpu.with_memory_space_constraint(v, pltpu.HBM) for v in ins])


X, C, Z0, Z1, SIDE = range(5)


def rows_at(start, size):
    return pl.ds(pl.multiple_of(start, 16), size)


def head_lanes():
    return lax.broadcasted_iota(jnp.int32, (TILE, PAIR), 1) < HEAD_DIM


def both_heads(block):
    first = head_lanes()
    zero = jnp.zeros_like(block)
    return jnp.concatenate([jnp.where(first, block, zero), jnp.where(first, zero, block)], axis=0)


def side_by_side(stacked):
    return jnp.where(head_lanes(), stacked[:TILE], stacked[TILE:])


def project(x, w, bias, q, k, v):
    q[...] = (dot(x[...], w[0]) + bias[0]).astype(bf16)
    k[...] = dot(x[...], w[1]).astype(bf16)
    v[...] = (dot(x[...], w[2]) + bias[1]).astype(bf16)


def attention(mask, q, k, v, probs, ctx):
    tokens, width = q.shape
    pairs = width // PAIR
    for t in range(tokens // TILE):
        rows = pl.ds(t * TILE, TILE)
        bias = mask[t]
        bias = jnp.concatenate([bias, bias], axis=0)
        for p in range(pairs):
            lanes = pl.ds(p * PAIR, PAIR)
            queries = both_heads(q[rows, lanes] * jnp.asarray(SCALE, bf16))
            scores = dot(queries, k[rows, lanes], NT) + bias
            raised = jnp.exp(scores - jnp.max(scores, axis=-1, keepdims=True))
            prob = (raised / jnp.sum(raised, axis=-1, keepdims=True)).astype(bf16)
            probs[t * pairs + p] = prob
            ctx[rows, lanes] = side_by_side(dot(prob, v[rows, lanes])).astype(bf16)


def attend_own(me, x, w, bias, mask, q, k, v, probs, ctx, x_t):
    x_t[...] = x[...].T
    project(x, w, bias, q, k, v)
    attention(mask, q, k, v, probs, ctx)


def normed(z):
    centred = z - jnp.mean(z, axis=-1, keepdims=True)
    inv = lax.rsqrt(jnp.mean(centred * centred, axis=-1, keepdims=True) + EPS)
    return centred * inv, inv


def norm_back(grad_normed, n, inv):
    return inv * (
        grad_normed
        - jnp.mean(grad_normed, axis=-1, keepdims=True)
        - n * jnp.mean(grad_normed * n, axis=-1, keepdims=True)
    )


def attn_copies(piece, core, w_qkv, w_out, out, sems, first):
    rows = w_qkv.shape[1] // 8
    half = w_qkv.shape[2]
    out_rows = w_out.shape[0] // 8
    mine = w_out.at[rows_at((2 * piece + core) * out_rows, out_rows)]
    pairs = (
        (w_qkv.at[:, rows_at((2 * piece + core) * rows, rows), :], out.at[0:3]),
        (mine.at[:, 0:half], out.at[3, 0:out_rows]),
        (mine.at[:, half : 2 * half], out.at[3, out_rows : 2 * out_rows]),
    )
    return [pltpu.make_async_copy(a, b, sems.at[first + i]) for i, (a, b) in enumerate(pairs)]


def feed_copies(piece, core, w_in, w_back, out, sems, first):
    model, hidden = w_in.shape
    width, rows = hidden // 4, model // 2
    half = width // 2
    mine = w_back.at[rows_at(piece * width + core * half, half)]
    pairs = (
        (w_in.at[rows_at(core * rows, rows), pl.ds(pl.multiple_of(piece * width, 128), width)], out.at[0:rows]),
        (mine.at[:, 0:width], out.at[rows : rows + half]),
        (mine.at[:, width : 2 * width], out.at[rows + half : rows + 2 * half]),
    )
    return [pltpu.make_async_copy(a, b, sems.at[first + i]) for i, (a, b) in enumerate(pairs)]


def run_copies(copies):
    for copy in copies:
        copy.start()
    for copy in copies:
        copy.wait()


def pack_attn(opposite, me, w_qkv, w_out, out, sems):
    piece = 2 * me[X] + me[Z0]
    run_copies(attn_copies(3 - piece if opposite else piece, me[C], w_qkv, w_out, out, sems, 0))


def pack_feed(opposite, me, w_in, w_back, out, sems):
    piece = 2 * me[X] + me[Z0]
    run_copies(feed_copies(3 - piece if opposite else piece, me[C], w_in, w_back, out, sems, 0))


def pack_biases(me, attn_bias, ffn_bias, biases):
    width = biases.shape[2]
    for i in range(2):
        biases[i] = attn_bias[i : i + 1]
    for i in range(4):
        biases[2 + i] = ffn_bias[pl.ds(i * width, width)].reshape(1, width)


def attend_other(
    me, x, n0, n1_, n2, n3, c0, c1, c2, c3, bias, mask, ctx_own, wo_own, res_bias, gains, shifts,
    q, k, v, probs, ctx, w, wo_all, mid, mid_low, n1, r1,
):
    core = me[C]
    rows = n0.shape[1]
    half = wo_all.shape[1] // 2
    part = rows // 2
    for r, (near, across) in enumerate(((n0, c0), (n1_, c1), (n2, c2), (n3, c3))):
        piece = (2 * me[X] + me[Z0]) ^ r
        for c, block in ((core, near), (1 - core, across)):
            w[:, rows_at((2 * piece + c) * rows, rows), :] = block[0:3]
            wo_all[rows_at((2 * piece + c) * part, part), 0:half] = block[3, 0:part]
            wo_all[rows_at((2 * piece + c) * part, part), half : 2 * half] = block[3, part : 2 * part]
    project(x, w, bias, q, k, v)
    attention(mask, q, k, v, probs, ctx)
    attended = dot(ctx_own[...], wo_own[...]) + dot(ctx[...], wo_all[...]) + res_bias[0:1]
    n_one, inv = normed(x[...].astype(f32) + attended)
    n1[...] = n_one
    r1[...] = inv
    value = n_one * gains[0:1] + shifts[0:1]
    mid[...] = value
    mid_low[...] = value.astype(bf16)


def gelu_both(a):
    cdf = 0.5 * (1.0 + lax.erf(a * inv_root_two))
    return a * cdf, cdf + a * jnp.exp(-0.5 * a * a) * inv_root_tau


def feed_own(me, mid_low, w_in, bias, w_back, hidden, slope, total, mid_t):
    row = jnp.concatenate([bias[2 + i] for i in range(4)], axis=1)
    value, grad = gelu_both(dot(mid_low[...], w_in[...]) + row)
    value = value.astype(bf16)
    hidden[...] = value
    slope[...] = grad.astype(bf16)
    total[...] = dot(value, w_back[...])
    mid_t[...] = mid_low[...].T


def feed_other(
    me, mid_low, bias, f0, f1, f2, f3, c0, c1, c2, c3, total, mid, cotangent, res_bias, gains, shifts,
    hidden, slope, w_in, w_back, output, grad_two, fed, sums,
):
    core = me[C]
    model = w_in.shape[0]
    width = w_in.shape[1] // 4
    rows, half = model // 2, width // 2
    for r, (near, across) in enumerate(((f0, c0), (f1, c1), (f2, c2), (f3, c3))):
        for c, block in ((core, near), (1 - core, across)):
            w_in[rows_at(c * rows, rows), r * width : (r + 1) * width] = block[0:rows]
            to = rows_at(r * width + c * half, half)
            w_back[to, 0:width] = block[rows : rows + half]
            w_back[to, width : 2 * width] = block[rows + half : rows + 2 * half]
    row = jnp.concatenate([bias[2 + ((2 * me[X] + me[Z0]) ^ r)] for r in range(4)], axis=1)
    value, grad = gelu_both(dot(mid_low[...], w_in[...]) + row)
    value = value.astype(bf16)
    hidden[...] = value
    slope[...] = grad.astype(bf16)
    ffn = total[...] + res_bias[1:2] + dot(value, w_back[...])
    n2, inv = normed(mid[...] + ffn)
    output[...] = (n2 * gains[1:2] + shifts[1:2]).astype(bf16)
    g = cotangent[...].astype(f32)
    grad = norm_back(g * gains[1:2], n2, inv)
    grad_two[...] = grad
    low = grad.astype(bf16)
    fed[...] = low
    sums[0:1] = jnp.sum(low.astype(f32), axis=0, keepdims=True)
    sums[1:2] = jnp.sum(g * n2, axis=0, keepdims=True)
    sums[2:3] = jnp.sum(g, axis=0, keepdims=True)


def slot(core, own_or_other, rx, r0):
    first = core == 0
    return jnp.where(first, own_or_other, r0), jnp.where(first, rx, own_or_other), jnp.where(first, r0, rx)


def relative(me, h, quarter):
    if h:
        return quarter // 2, quarter % 2
    return me[X] ^ (quarter // 2), me[Z0] ^ (quarter % 2)


def back_grad(me, hid_own, hid_other, fed, away, keep, grads):
    core = me[C]
    width = hid_own.shape[1] // 4
    size = width // 4
    for h, hid in enumerate((hid_own, hid_other)):
        grads[h] = dot(hid[...], fed[...], TN).astype(bf16)
        for q in range(4):
            rx, r0 = relative(me, h, q)
            for c, out in ((1 - core, away), (core, keep)):
                for j in range(2):
                    out[*slot(c, h, rx, r0), j] = grads[h, rows_at(q * width + (2 * c + j) * size, size), :]


def in_grad(mid_t, fed, w_back, slope, w_in, bias_sums, place):
    pre = (dot(fed[...], w_back[...], NT) * slope[...].astype(f32)).astype(bf16)
    width = pre.shape[1] // 4
    sums = jnp.sum(pre.astype(f32), axis=0, keepdims=True)
    for q in range(4):
        bias_sums[place(q)] = sums[:, q * width : (q + 1) * width]
    return dot(mid_t[...], pre).astype(bf16), dot(pre, w_in[...], NT)


def in_grad_own(me, mid_t, fed, w_back, slope, w_in, grads, bias_sums, total):
    grads[...], total[...] = in_grad(mid_t, fed, w_back, slope, w_in, bias_sums, lambda q: q)


def in_grad_other(
    me, mid_t, fed, w_back, slope, w_in, grads_own, total_own, grad_two, n1, r1, gains,
    away, keep, bias_sums, grad_one, grad_att, sums, grads,
):
    core, here = me[C], 2 * me[X] + me[Z0]
    grads[...], part = in_grad(mid_t, fed, w_back, slope, w_in, bias_sums, lambda q: here ^ q)
    width = w_in.shape[1] // 4
    size = w_in.shape[0] // 4
    for h, source in ((0, grads_own), (1, grads)):
        for q in range(4):
            rx, r0 = relative(me, h, q)
            for c, out in ((1 - core, away), (core, keep)):
                for j in range(2):
                    out[*slot(c, h, rx, r0), j] = source[
                        rows_at((2 * c + j) * size, size), q * width : (q + 1) * width
                    ]
    grad_mid = grad_two[...] + total_own[...] + part
    n = n1[...]
    sums[1:2] = jnp.sum(grad_mid * n, axis=0, keepdims=True)
    sums[2:3] = jnp.sum(grad_mid, axis=0, keepdims=True)
    grad = norm_back(grad_mid * gains[0:1], n, r1[...])
    grad_one[...] = grad
    low = grad.astype(bf16)
    grad_att[...] = low
    sums[0:1] = jnp.sum(low.astype(f32), axis=0, keepdims=True)


def attend_back(me, grad_att, w_out, ctx, q, k, v, probs, grads, grad_out, gctx):
    half = grad_out.shape[2]
    gctx[...] = dot(grad_att[...], w_out[...], NT).astype(bf16)
    grad = dot(ctx[...], grad_att[...], TN).astype(bf16)
    grad_out[0] = grad[:, :half]
    grad_out[1] = grad[:, half:]
    tokens, width = q.shape
    pairs = width // PAIR
    for t in range(tokens // TILE):
        rows = pl.ds(t * TILE, TILE)
        for p in range(pairs):
            lanes = pl.ds(p * PAIR, PAIR)
            prob = probs[t * pairs + p]
            context = both_heads(gctx[rows, lanes])
            grads[rows, pl.ds(2 * width + p * PAIR, PAIR)] = dot(prob, context, TN).astype(bf16)
            grad_prob = dot(context, v[rows, lanes], NT)
            prob = prob.astype(f32)
            mean = jnp.sum(prob * grad_prob, axis=-1, keepdims=True)
            score = (prob * (grad_prob - mean)).astype(bf16)
            grads[rows, lanes] = (side_by_side(dot(score, k[rows, lanes])) * SCALE).astype(bf16)
            queries = both_heads(q[rows, lanes])
            grads[rows, pl.ds(width + p * PAIR, PAIR)] = (dot(score, queries, TN) * SCALE).astype(bf16)


def qkv_grad(
    me, x_t, own, own_out, oth, oth_out, sums_one, sums_two, ffn_own, ffn_other, away, keep, grads, small,
):
    mx, mc, m0 = me[X], me[C], me[Z0]
    half = keep.shape[5]
    size = half // 8
    small[...] = jnp.zeros_like(small)
    for h, g, out, ffn in ((0, own, own_out, ffn_own), (1, oth, oth_out, ffn_other)):
        grads[h] = dot(x_t[...], g[...]).astype(bf16)
        rows = [s[i : i + 1, j * half : (j + 1) * half] for s in (sums_one, sums_two) for i in range(3) for j in range(2)]
        rows += [ffn[i] for i in range(4)]
        rows += [
            jnp.sum(g[:, c * half : (c + 1) * half].astype(f32), axis=0, keepdims=True) for c in (0, 2)
        ]
        for i, row in enumerate(rows):
            small[h, i // 2, i % 2 : i % 2 + 1] = row
        for core, piece in ((1 - mc, away), (mc, keep)):
            for rx in range(2):
                for r0 in range(2):
                    place = 4 * core + 2 * (mx ^ rx) + (m0 ^ r0)
                    for j in range(2):
                        to = (*slot(core, h, rx, r0), j)
                        for c in range(3):
                            piece[*to, c * size : (c + 1) * size, :] = grads[
                                h, rows_at(size * (2 * place + j), size), c * half : (c + 1) * half
                            ]
                        piece[*to, 3 * size : 4 * size, :] = out[j, rows_at(size * place, size), :]
                        piece[*to, 4 * size : 4 * size + 16, :] = split(small[h, 2 * place + j])


def split(values):
    high = values.astype(bf16).astype(f32)
    rest = values - high
    middle = rest.astype(bf16).astype(f32)
    fill = jnp.zeros((10, values.shape[1]), f32)
    return jnp.concatenate([high, middle, rest - middle, fill], axis=0).astype(bf16)


def joined(rows):
    rows = rows.astype(f32)
    return rows[0:2] + rows[2:4] + rows[4:6]


def token_grad(me, grad_one, own, oth, w_own, w_other, out):
    total = grad_one[...]
    half = w_own.shape[2]
    for g, w in ((own, w_own), (oth, w_other)):
        for c in range(3):
            total += dot(g[:, c * half : (c + 1) * half], w[c], NT)
    out[...] = total.astype(bf16)


def place_rows(by_rows, me, b0, b1, b2, b3, out):
    size, width = b0.shape[2:]
    for place in range(4):
        rx, r0 = me[X] ^ (place // 2), me[Z0] ^ (place % 2)
        for c, blocks in ((0, (b0, b2)), (1, (b1, b3))):
            core = me[C] ^ c
            for last, block in enumerate(blocks):

                @pl.when(jnp.where(core == 0, rx, r0) == last)
                def _():
                    for j in range(2):
                        start = (2 * core + j) * size
                        start = pl.multiple_of(start + place * 4 * size if by_rows else start, 8)
                        lanes = slice(0, width) if by_rows else slice(place * width, (place + 1) * width)
                        out[pl.ds(start, size), lanes] = block[jnp.where(core == 0, r0, rx), j].astype(f32)


def place_attn(me, b0, b1, b2, b3, qkv, w_out, attn_bias, res_bias, ffn_bias, gains, shifts, small):
    half = b0.shape[3]
    size = half // 8
    for c, blocks in ((0, (b0, b2)), (1, (b1, b3))):
        core = me[C] ^ c
        for last, block in enumerate(blocks):
            for inner in range(2):
                rx, r0 = jnp.where(core == 0, last, inner), jnp.where(core == 0, inner, last)
                start = 4 * core + 2 * (me[X] ^ rx) + (me[Z0] ^ r0)
                for j in range(2):
                    rows = pl.ds(pl.multiple_of((2 * start + j) * size, 8), size)
                    for n in range(3):
                        qkv[n, rows, :] = block[inner, j, n * size : (n + 1) * size].astype(f32)
                    rows = pl.ds(pl.multiple_of(start * size, 8), size)
                    w_out[rows, j * half : (j + 1) * half] = block[inner, j, 3 * size : 4 * size].astype(f32)
                    small[2 * start + j] = joined(block[inner, j, 4 * size : 4 * size + 16])
    row = lambda i: small[i // 2, i % 2 : i % 2 + 1]
    for out, first in ((res_bias, 0), (gains, 2), (shifts, 4)):
        for i in range(2):
            for j in range(2):
                out[i : i + 1, j * half : (j + 1) * half] = row(first + 6 * i + j)
    for i in range(4):
        ffn_bias[pl.ds(i * half, half)] = row(12 + i).reshape(half)
    for i in range(2):
        attn_bias[i : i + 1] = row(16 + i)


def add_parts(places, small, me, *refs):
    *ins, out = refs
    lead = out.shape[:-2]
    for i in range(math.prod(lead)):
        at = tuple(int(v) for v in np.unravel_index(i, lead))
        total = ins[0][(*places[0], *at)].astype(f32)
        for place, part in zip(places[1:], ins[1:]):
            total += part[(*place, *at)].astype(f32)
        if small:
            n = out.shape[-2] - 16
            tails = [part[(*place, *at)][n:] for place, part in zip(places, ins)]
            out[(*at, slice(0, n))] = total[:n].astype(out.dtype)
            out[(*at, slice(n, n + 16))] = split(sum(joined(t) for t in tails))
        else:
            out[at] = total.astype(out.dtype)


def join(me, a, b, out):
    out[0] = a[...]
    out[1] = b[...]


def tick(me, x, out):
    out[...] = x[...]


def choose(me, a, b, out):
    @pl.when(me[C] == 0)
    def _():
        out[...] = a[...]

    @pl.when(me[C] == 1)
    def _():
        out[...] = b[...]


def mask_bias(bucket, length_row, side, count):
    width = jnp.where(bucket == 0, 32, jnp.where(bucket == 1, 64, 128)).astype(jnp.int32)
    place = side * count + jnp.arange(count, dtype=jnp.int32)
    slot = place // width
    inside = place - slot * width
    match = slot[:, None] == jnp.arange(length_row.shape[0], dtype=jnp.int32)[None, :]
    length = jnp.sum(jnp.where(match, length_row[None, :], 0), axis=1)
    slot, key_ok = slot.reshape(-1, TILE), (inside < length).reshape(-1, TILE)
    same = slot[:, :, None] == slot[:, None, :]
    return jnp.where(same & key_ok[:, None, :], 0.0, NEG).astype(f32)


ORDER = (
    "back", "in1", "B_S0", "in2", "ab1", "I_S0", "ab2", "qkv+B_p0", "B_S1", "A_S0", "I_S1", "B_S2",
    "tok", "B_S3", "I_S2", "A_S1", "B_A0", "A_S2", "I_S3", "A_S3+B_g0", "B_A1", "I_A0", "A_A0+B_gc",
    "I_A1", "A_A1", "B_P+I_gc", "I_P+A_gc", "A_P",
)
def per_device(
    dp_size, tokens, w_qkv, attn_bias, w_out, res_bias, w_in, ffn_bias, w_back,
    norm_gains, norm_shifts, cotangent, buckets, lengths,
):
    here = lax.axis_index("dp")
    side = lax.axis_index("tensor")
    n_bits = dp_size.bit_length() - 1
    assert 1 << n_bits == dp_size and n_bits >= 4

    def bit(b):
        return (here >> b) & 1

    me = jnp.stack([bit(1), bit(0), bit(2), bit(3), side]).astype(jnp.int32)

    def over_dp(value, b):
        return lax.ppermute(value, "dp", [(i, i ^ (1 << b)) for i in range(dp_size)])

    def over_tensor(value):
        return lax.ppermute(value, "tensor", [(0, 1), (1, 0)])

    y, x, z0, z1 = 1, 4, 8, 16
    reduce_steps = (y, z0), (x, y), (z0, x)
    gather_steps = (z0, x), (x, z0)

    def flip(value, partners):
        pairs = [(i, i ^ partners[(i >> 1) & 1]) for i in range(2 * dp_size)]
        return lax.ppermute(value, ("dp", "tensor"), pairs)

    n_tokens, model = tokens.shape
    half = w_qkv.shape[2]
    hidden_half = w_in.shape[1]
    quarter = hidden_half // 4
    n_units = n_tokens // TILE * (half // PAIR)

    def after(value, *others):
        return lax.optimization_barrier((value, *others))[0]

    clock = [me]
    waits = []

    def step(body, *inputs, wait=()):
        flat, tree = jax.tree.flatten(inputs)
        held = lax.optimization_barrier((*flat, clock[0], *jax.tree.leaves(wait), *waits))
        waits.clear()
        out = body(*jax.tree.unflatten(tree, held[: len(flat)]))
        clock[0] = jax.tree.leaves(out)[0]
        return out

    def kernel(body, name, ins, outs, scratch=(), wait=(), cost=COST):
        return step(lambda *a: call(body, name, me, a, outs, scratch=scratch, cost=cost), *ins, wait=wait)

    near_shape = sds((4, model // 8, half))
    feed_shape = sds((model, quarter))
    near, = packed(functools.partial(pack_attn, False), "pack_near", me, (w_qkv, w_out), [near_shape])
    near_y = over_tensor(near)
    clock[0] = near
    biases, = kernel(pack_biases, "pack_biases", (attn_bias, ffn_bias), [sds((6, 1, quarter), f32)])
    biases_other = over_tensor(biases)

    def pack(body, name, opposite, weights, shape, wait=()):
        out, = step(
            lambda *w: packed(functools.partial(body, opposite), name, me, w, [shape]), *weights, wait=wait
        )
        return over_tensor(out)

    feed_y = pack(pack_feed, "pack_feed", False, (w_in, w_back), feed_shape)
    near_z, near_x = over_dp(near_y, 2), over_dp(near_y, 1)
    mask = step(lambda b, l: mask_bias(b, l, side, n_tokens), buckets[0], lengths[0])

    act = sds((n_tokens, half))
    probs = sds((n_units, 2 * TILE, TILE))
    wide = sds((n_tokens, model), f32)
    column = sds((n_tokens, 1), f32)
    own_q, own_k, own_v, own_p, own_ctx, tokens_t = kernel(
        attend_own, "attend_own", (tokens, w_qkv, biases, mask),
        [act, act, act, probs, act, sds((model, n_tokens))], cost=LITTLE,
    )
    near_c = [over_dp(after(v, own_ctx), 0) for v in (near_y, near_z, near_x)]
    passed, = kernel(choose, "choose", (near_z, near_x), [near_shape])
    near_d = flip(passed, (x, z0))
    feed_z, feed_x = over_dp(feed_y, 2), over_dp(feed_y, 1)
    turn, = kernel(tick, "tick", (mask[0, :8],), [sds((8, TILE), f32)], wait=(feed_y, biases_other, *near_c))
    feed_d_y = pack(pack_feed, "pack_feed_d", True, (w_in, w_back), feed_shape)
    near_all = near_y, near_z, near_x, near_d
    near_c.append(over_dp(after(near_d, turn), 0))
    (oth_q, oth_k, oth_v, oth_p, oth_ctx, w_qkv_other, w_out_other, mid, mid_low, n1, r1) = kernel(
        attend_other, "attend_other",
        (tokens, *near_all, *near_c, biases_other, mask, own_ctx, w_out,
         res_bias, norm_gains, norm_shifts),
        [act, act, act, probs, act, sds(w_qkv.shape), sds(w_out.shape), wide, sds(tokens.shape), wide, column],
        cost=LITTLE,
    )

    hidden_own, slope_own, total_own, mid_t = kernel(
        feed_own, "feed_own", (mid_low, w_in, biases, w_back),
        [sds((n_tokens, hidden_half)), sds((n_tokens, hidden_half)), wide, sds((model, n_tokens))],
        wait=feed_y, cost=LITTLE,
    )
    feed_all = feed_y, feed_z, feed_x, feed_d_y
    feed_c = [over_dp(after(feed_y, mid_low), 0)] + [over_dp(after(v, total_own), 0) for v in feed_all[1:]]
    (hidden_other, slope_other, w_in_other, w_back_other, output, grad_two, fed, sums_two) = kernel(
        feed_other, "feed_other",
        (mid_low, biases_other, *feed_all, *feed_c, total_own, mid, cotangent,
         res_bias, norm_gains, norm_shifts),
        [sds((n_tokens, hidden_half)), sds((n_tokens, hidden_half)), sds(w_in.shape),
         sds(w_back.shape), sds(tokens.shape), wide, sds(tokens.shape), sds((3, model), f32)],
    )

    env = {}
    ops = {}
    flying = {}

    def sent(key, value):
        flying[key] = value
        return value

    def chain(name, finish):
        state = {}

        def add(name_of, parts, places, shape):
            body = functools.partial(add_parts, places, name == "A")
            return kernel(body, name_of, parts, [sds(shape)])[0]

        def reduce(i):
            def run():
                if i == 0:
                    state["parts"], state["places"] = list(env[name]), [(), ()]
                parts, places = state["parts"], state["places"]
                value = add("add_half", parts, [(*p, 1) for p in places], parts[0].shape[i + 1 :])
                parts.append(sent(f"{name}_p{i}", flip(value, reduce_steps[i])))
                state["places"] = [(*p, 0) for p in places] + [()]

            return run

        def exchange():
            value = add("add_all", state["parts"], state["places"], state["parts"][-1].shape)
            state["pair"] = value, sent(name + "_p3", flip(value, (z1, z1)))

        def gather(i):
            def run():
                pair = state["pair"]
                if i == 0:
                    value = add("add_two", pair, [(), ()], pair[0].shape)
                    for b in range(4, n_bits):
                        value = add("add_two", (value, over_dp(value, b)), [(), ()], value.shape)
                else:
                    value, = kernel(join, "join", pair, [sds((2, *pair[0].shape))])
                got = sent(f"{name}_g{i}", flip(value, gather_steps[i]))
                state["pair"] = value, got
                if i == 1:
                    value_c = sent(name + "_gc", over_dp(value, 0))
                    state["blocks"] = value, value_c, got
                    if name != "A":
                        core_end()

            return run

        for i in range(3):
            ops[f"{name}_S{i}"] = reduce(i)
        ops[name + "_S3"] = exchange
        for i in range(2):
            ops[f"{name}_A{i}"] = gather(i)

        def core_end():
            got = state["blocks"][2]
            state["blocks"] = *state["blocks"], over_dp(after(got, clock[0]) if name == "A" else got, 0)

        def place():
            if name == "A":
                core_end()
            env[name + "_result"] = finish(state["blocks"])

        ops[name + "_P"] = place

    sub = quarter // 4
    piece = sds((2, 2, 2, 2, sub, model))
    in_piece = sds((2, 2, 2, 2, model // 4, quarter))
    attn_piece = sds((2, 2, 2, 2, half // 2 + 16, half))
    raw_out = sds((2, half, model // 2))

    def back():
        away, keep = kernel(
            back_grad, "back_grad", (hidden_own, hidden_other, fed), [piece, piece],
            scratch=[pltpu.VMEM((2, hidden_half, model), bf16)],
        )
        env["B"] = keep, sent("B_c", over_dp(away, 0))

    def in_first():
        env["in_own"] = kernel(
            in_grad_own, "in_grad_own", (mid_t, fed, w_back, slope_own, w_in),
            [sds(w_in.shape), sds((4, 1, quarter), f32), wide],
        )

    def in_second():
        grads_own, bias_own, mid_own = env["in_own"]
        away, keep, bias_other, grad_one, grad_att, sums_one = kernel(
            in_grad_other, "in_grad_other",
            (mid_t, fed, w_back_other, slope_other, w_in_other, grads_own, mid_own, grad_two, n1, r1, norm_gains),
            [in_piece, in_piece, sds((4, 1, quarter), f32), wide, sds(tokens.shape), sds((3, model), f32)],
            scratch=[pltpu.VMEM(w_in.shape, bf16)],
        )
        env["I"] = keep, sent("I_c", over_dp(away, 0))
        env.update(bias_own=bias_own, bias_other=bias_other, grad_one=grad_one, grad_att=grad_att, sums_one=sums_one)

    def attn_back(w, ctx, q, k, v, p):
        return kernel(
            attend_back, "attend_back", (env["grad_att"], w, ctx, q, k, v, p),
            [sds((n_tokens, 3 * half)), raw_out],
            scratch=[pltpu.VMEM((n_tokens, half), bf16)],
        )

    def attn_first():
        env["own"] = attn_back(w_out, own_ctx, own_q, own_k, own_v, own_p)

    def attn_second():
        env["other"] = attn_back(w_out_other, oth_ctx, oth_q, oth_k, oth_v, oth_p)

    def qkv():
        away, keep = kernel(
            qkv_grad, "qkv_grad",
            (tokens_t, *env["own"], *env["other"], env["sums_one"], sums_two, env["bias_own"], env["bias_other"]),
            [attn_piece, attn_piece],
            scratch=[pltpu.VMEM((2, model, 3 * half), bf16), pltpu.VMEM((2, 16, 2, half), f32)],
        )
        env["A"] = keep, sent("A_c", over_dp(away, 0))

    def token():
        env["grad_tokens"], = kernel(
            token_grad, "token_grad", (env["grad_one"], env["own"][0], env["other"][0], w_qkv, w_qkv_other), [sds(tokens.shape)]
        )

    chain("B", lambda blocks: kernel(
        functools.partial(place_rows, True), "place_back", blocks, [sds(w_back.shape, f32)]
    ))
    chain("I", lambda blocks: kernel(
        functools.partial(place_rows, False), "place_in", blocks, [sds(w_in.shape, f32)]
    ))
    last_shapes = [w_qkv.shape, w_out.shape, (2, half), (2, model), (hidden_half,), (2, model), (2, model)]
    chain("A", lambda blocks: kernel(
        place_attn, "place_attn", blocks, [sds(shape, f32) for shape in last_shapes],
        scratch=[pltpu.VMEM((16, 2, half), f32)],
    ))
    ops.update({
        "back": back, "in1": in_first, "in2": in_second, "ab1": attn_first, "ab2": attn_second,
        "qkv": qkv, "tok": token,
    })
    for entry in ORDER:
        key, *ended = entry.split("+")
        waits.extend(flying.pop(p) for p in ended)
        ops.pop(key)()
    assert not ops
    grad_tokens = env["grad_tokens"]
    (grad_back,), (grad_in,) = env["B_result"], env["I_result"]
    grad_qkv, grad_out, grad_attn_bias, grad_res_bias, grad_ffn_bias, grad_gains, grad_shifts = env["A_result"]

    return (
        output,
        grad_tokens,
        grad_qkv,
        grad_attn_bias,
        grad_out,
        grad_res_bias,
        grad_in,
        grad_ffn_bias,
        grad_back,
        grad_gains,
        grad_shifts,
    )


def solution(mesh):
    dp_size = mesh.shape["dp"]
    placed = (
        P(("dp", "tensor"), None),
        P(None, None, "tensor"),
        P(None, "tensor"),
        P("tensor", None),
        P(),
        P(None, "tensor"),
        P("tensor"),
        P("tensor", None),
        P(),
        P(),
        P(("dp", "tensor"), None),
        P("dp"),
        P("dp", None),
    )
    return jax.shard_map(
        lambda *args: per_device(dp_size, *args),
        mesh=mesh,
        in_specs=placed,
        out_specs=(
            P(("dp", "tensor"), None),
            P(("dp", "tensor"), None),
            P(None, None, "tensor"),
            P(None, "tensor"),
            P("tensor", None),
            P(),
            P(None, "tensor"),
            P("tensor"),
            P("tensor", None),
            P(),
            P(),
        ),
        check_vma=False,
    )
```

```python
import functools
import math

import jax
import jax.numpy as jnp
import numpy as np
from jax import lax
from jax.experimental import pallas as pl
from jax.experimental.pallas import tpu as pltpu
from jax.sharding import PartitionSpec as P

HEAD_DIM = 64
ROW_LEN = 1024
TILE = 128
PAIR = 2 * HEAD_DIM
NEG = -1000000000.0
EPS = 1e-05
SCALE = HEAD_DIM ** (-0.5)
inv_root_two = 1.0 / math.sqrt(2.0)
inv_root_tau = 1.0 / math.sqrt(2.0 * math.pi)
f32 = jnp.float32
bf16 = jnp.bfloat16
MB = 1 << 20
LIMIT = 12
WIDE_LIMIT = 14
WIDE = {"feed_own", "feed_other", "back_grad", "in_grad_own", "in_grad_other", "qkv_grad"}

NN, NT, TN = ((1,), (0,)), ((1,), (1,)), ((0,), (0,))


def dot(a, b, dims=NN):
    return lax.dot_general(a, b, (dims, ((), ())), preferred_element_type=f32)


def sds(shape, dtype=bf16):
    return jax.ShapeDtypeStruct(shape, dtype)


def vmem():
    return pl.BlockSpec(memory_space=pltpu.VMEM)


def smem():
    return pl.BlockSpec(memory_space=pltpu.SMEM)


COST = pl.CostEstimate(flops=3 * 10**10, bytes_accessed=10**15, transcendentals=0)


LITTLE = pl.CostEstimate(flops=1, bytes_accessed=10**15, transcendentals=0)


def call(body, name, me, ins, outs, scratch=(), cost=COST):
    limit = WIDE_LIMIT if name in WIDE else LIMIT
    return pl.pallas_call(
        body,
        name=name,
        out_shape=outs,
        in_specs=[smem()] + [vmem()] * len(ins),
        out_specs=[vmem()] * len(outs),
        scratch_shapes=scratch,
        compiler_params=pltpu.CompilerParams(vmem_limit_bytes=limit * MB),
        cost_estimate=cost,
    )(me, *ins)


def packed(body, name, me, ins, outs):
    return pl.pallas_call(
        body,
        name=name,
        out_shape=outs,
        in_specs=[smem()] + [pl.BlockSpec(memory_space=pltpu.HBM)] * len(ins),
        out_specs=[vmem()] * len(outs),
        scratch_shapes=[pltpu.SemaphoreType.DMA((3,))],
        compiler_params=pltpu.CompilerParams(vmem_limit_bytes=LIMIT * MB),
        cost_estimate=COST,
    )(me, *[pltpu.with_memory_space_constraint(v, pltpu.HBM) for v in ins])


X, C, Z0, Z1, SIDE = range(5)


def rows_at(start, size):
    return pl.ds(pl.multiple_of(start, 16), size)


def head_lanes():
    return lax.broadcasted_iota(jnp.int32, (TILE, PAIR), 1) < HEAD_DIM


def both_heads(block):
    first = head_lanes()
    zero = jnp.zeros_like(block)
    return jnp.concatenate([jnp.where(first, block, zero), jnp.where(first, zero, block)], axis=0)


def side_by_side(stacked):
    return jnp.where(head_lanes(), stacked[:TILE], stacked[TILE:])


def project(x, w, bias, q, k, v):
    q[...] = (dot(x[...], w[0]) + bias[0]).astype(bf16)
    k[...] = dot(x[...], w[1]).astype(bf16)
    v[...] = (dot(x[...], w[2]) + bias[1]).astype(bf16)


def attention(mask, q, k, v, probs, ctx):
    tokens, width = q.shape
    pairs = width // PAIR
    for t in range(tokens // TILE):
        rows = pl.ds(t * TILE, TILE)
        bias = mask[t]
        bias = jnp.concatenate([bias, bias], axis=0)
        for p in range(pairs):
            lanes = pl.ds(p * PAIR, PAIR)
            queries = both_heads(q[rows, lanes] * jnp.asarray(SCALE, bf16))
            scores = dot(queries, k[rows, lanes], NT) + bias
            raised = jnp.exp(scores - jnp.max(scores, axis=-1, keepdims=True))
            prob = (raised / jnp.sum(raised, axis=-1, keepdims=True)).astype(bf16)
            probs[t * pairs + p] = prob
            ctx[rows, lanes] = side_by_side(dot(prob, v[rows, lanes])).astype(bf16)


def attend_own(me, x, w, bias, mask, q, k, v, probs, ctx, x_t):
    x_t[...] = x[...].T
    project(x, w, bias, q, k, v)
    attention(mask, q, k, v, probs, ctx)


def normed(z):
    centred = z - jnp.mean(z, axis=-1, keepdims=True)
    inv = lax.rsqrt(jnp.mean(centred * centred, axis=-1, keepdims=True) + EPS)
    return centred * inv, inv


def norm_back(grad_normed, n, inv):
    return inv * (
        grad_normed
        - jnp.mean(grad_normed, axis=-1, keepdims=True)
        - n * jnp.mean(grad_normed * n, axis=-1, keepdims=True)
    )


def attn_copies(piece, core, w_qkv, w_out, out, sems, first):
    rows = w_qkv.shape[1] // 8
    half = w_qkv.shape[2]
    out_rows = w_out.shape[0] // 8
    mine = w_out.at[rows_at((2 * piece + core) * out_rows, out_rows)]
    pairs = (
        (w_qkv.at[:, rows_at((2 * piece + core) * rows, rows), :], out.at[0:3]),
        (mine.at[:, 0:half], out.at[3, 0:out_rows]),
        (mine.at[:, half : 2 * half], out.at[3, out_rows : 2 * out_rows]),
    )
    return [pltpu.make_async_copy(a, b, sems.at[first + i]) for i, (a, b) in enumerate(pairs)]


def feed_copies(piece, core, w_in, w_back, out, sems, first):
    model, hidden = w_in.shape
    width, rows = hidden // 4, model // 2
    half = width // 2
    mine = w_back.at[rows_at(piece * width + core * half, half)]
    pairs = (
        (w_in.at[rows_at(core * rows, rows), pl.ds(pl.multiple_of(piece * width, 128), width)], out.at[0:rows]),
        (mine.at[:, 0:width], out.at[rows : rows + half]),
        (mine.at[:, width : 2 * width], out.at[rows + half : rows + 2 * half]),
    )
    return [pltpu.make_async_copy(a, b, sems.at[first + i]) for i, (a, b) in enumerate(pairs)]


def run_copies(copies):
    for copy in copies:
        copy.start()
    for copy in copies:
        copy.wait()


def pack_attn(opposite, me, w_qkv, w_out, out, sems):
    piece = 2 * me[X] + me[Z0]
    run_copies(attn_copies(3 - piece if opposite else piece, me[C], w_qkv, w_out, out, sems, 0))


def pack_feed(opposite, me, w_in, w_back, out, sems):
    piece = 2 * me[X] + me[Z0]
    run_copies(feed_copies(3 - piece if opposite else piece, me[C], w_in, w_back, out, sems, 0))


def pack_biases(me, attn_bias, ffn_bias, biases):
    width = biases.shape[2]
    for i in range(2):
        biases[i] = attn_bias[i : i + 1]
    for i in range(4):
        biases[2 + i] = ffn_bias[pl.ds(i * width, width)].reshape(1, width)


def attend_other(
    me, x, n0, n1_, n2, n3, c0, c1, c2, c3, bias, mask, ctx_own, wo_own, res_bias, gains, shifts,
    q, k, v, probs, ctx, w, wo_all, mid, mid_low, n1, r1,
):
    core = me[C]
    rows = n0.shape[1]
    half = wo_all.shape[1] // 2
    part = rows // 2
    for r, (near, across) in enumerate(((n0, c0), (n1_, c1), (n2, c2), (n3, c3))):
        piece = (2 * me[X] + me[Z0]) ^ r
        for c, block in ((core, near), (1 - core, across)):
            w[:, rows_at((2 * piece + c) * rows, rows), :] = block[0:3]
            wo_all[rows_at((2 * piece + c) * part, part), 0:half] = block[3, 0:part]
            wo_all[rows_at((2 * piece + c) * part, part), half : 2 * half] = block[3, part : 2 * part]
    project(x, w, bias, q, k, v)
    attention(mask, q, k, v, probs, ctx)
    attended = dot(ctx_own[...], wo_own[...]) + dot(ctx[...], wo_all[...]) + res_bias[0:1]
    n_one, inv = normed(x[...].astype(f32) + attended)
    n1[...] = n_one
    r1[...] = inv
    value = n_one * gains[0:1] + shifts[0:1]
    mid[...] = value
    mid_low[...] = value.astype(bf16)


def gelu_both(a):
    cdf = 0.5 * (1.0 + lax.erf(a * inv_root_two))
    return a * cdf, cdf + a * jnp.exp(-0.5 * a * a) * inv_root_tau


def feed_own(me, mid_low, w_in, bias, w_back, hidden, slope, total, mid_t):
    row = jnp.concatenate([bias[2 + i] for i in range(4)], axis=1)
    value, grad = gelu_both(dot(mid_low[...], w_in[...]) + row)
    value = value.astype(bf16)
    hidden[...] = value
    slope[...] = grad.astype(bf16)
    total[...] = dot(value, w_back[...])
    mid_t[...] = mid_low[...].T


def feed_other(
    me, mid_low, bias, f0, f1, f2, f3, c0, c1, c2, c3, total, mid, cotangent, res_bias, gains, shifts,
    hidden, slope, w_in, w_back, output, grad_two, fed, sums,
):
    core = me[C]
    model = w_in.shape[0]
    width = w_in.shape[1] // 4
    rows, half = model // 2, width // 2
    for r, (near, across) in enumerate(((f0, c0), (f1, c1), (f2, c2), (f3, c3))):
        for c, block in ((core, near), (1 - core, across)):
            w_in[rows_at(c * rows, rows), r * width : (r + 1) * width] = block[0:rows]
            to = rows_at(r * width + c * half, half)
            w_back[to, 0:width] = block[rows : rows + half]
            w_back[to, width : 2 * width] = block[rows + half : rows + 2 * half]
    row = jnp.concatenate([bias[2 + ((2 * me[X] + me[Z0]) ^ r)] for r in range(4)], axis=1)
    value, grad = gelu_both(dot(mid_low[...], w_in[...]) + row)
    value = value.astype(bf16)
    hidden[...] = value
    slope[...] = grad.astype(bf16)
    ffn = total[...] + res_bias[1:2] + dot(value, w_back[...])
    n2, inv = normed(mid[...] + ffn)
    output[...] = (n2 * gains[1:2] + shifts[1:2]).astype(bf16)
    g = cotangent[...].astype(f32)
    grad = norm_back(g * gains[1:2], n2, inv)
    grad_two[...] = grad
    low = grad.astype(bf16)
    fed[...] = low
    sums[0:1] = jnp.sum(low.astype(f32), axis=0, keepdims=True)
    sums[1:2] = jnp.sum(g * n2, axis=0, keepdims=True)
    sums[2:3] = jnp.sum(g, axis=0, keepdims=True)


def slot(core, own_or_other, rx, r0):
    first = core == 0
    return jnp.where(first, own_or_other, r0), jnp.where(first, rx, own_or_other), jnp.where(first, r0, rx)


def relative(me, h, quarter):
    if h:
        return quarter // 2, quarter % 2
    return me[X] ^ (quarter // 2), me[Z0] ^ (quarter % 2)


def back_grad(me, hid_own, hid_other, fed, away, keep, grads):
    core = me[C]
    width = hid_own.shape[1] // 4
    size = width // 4
    for h, hid in enumerate((hid_own, hid_other)):
        grads[h] = dot(hid[...], fed[...], TN).astype(bf16)
        for q in range(4):
            rx, r0 = relative(me, h, q)
            for c, out in ((1 - core, away), (core, keep)):
                for j in range(2):
                    out[*slot(c, h, rx, r0), j] = grads[h, rows_at(q * width + (2 * c + j) * size, size), :]


def in_grad(mid_t, fed, w_back, slope, w_in, bias_sums, place):
    pre = (dot(fed[...], w_back[...], NT) * slope[...].astype(f32)).astype(bf16)
    width = pre.shape[1] // 4
    sums = jnp.sum(pre.astype(f32), axis=0, keepdims=True)
    for q in range(4):
        bias_sums[place(q)] = sums[:, q * width : (q + 1) * width]
    return dot(mid_t[...], pre).astype(bf16), dot(pre, w_in[...], NT)


def in_grad_own(me, mid_t, fed, w_back, slope, w_in, grads, bias_sums, total):
    grads[...], total[...] = in_grad(mid_t, fed, w_back, slope, w_in, bias_sums, lambda q: q)


def in_grad_other(
    me, mid_t, fed, w_back, slope, w_in, grads_own, total_own, grad_two, n1, r1, gains,
    away, keep, bias_sums, grad_one, grad_att, sums, grads,
):
    core, here = me[C], 2 * me[X] + me[Z0]
    grads[...], part = in_grad(mid_t, fed, w_back, slope, w_in, bias_sums, lambda q: here ^ q)
    width = w_in.shape[1] // 4
    size = w_in.shape[0] // 4
    for h, source in ((0, grads_own), (1, grads)):
        for q in range(4):
            rx, r0 = relative(me, h, q)
            for c, out in ((1 - core, away), (core, keep)):
                for j in range(2):
                    out[*slot(c, h, rx, r0), j] = source[
                        rows_at((2 * c + j) * size, size), q * width : (q + 1) * width
                    ]
    grad_mid = grad_two[...] + total_own[...] + part
    n = n1[...]
    sums[1:2] = jnp.sum(grad_mid * n, axis=0, keepdims=True)
    sums[2:3] = jnp.sum(grad_mid, axis=0, keepdims=True)
    grad = norm_back(grad_mid * gains[0:1], n, r1[...])
    grad_one[...] = grad
    low = grad.astype(bf16)
    grad_att[...] = low
    sums[0:1] = jnp.sum(low.astype(f32), axis=0, keepdims=True)


def attend_back(me, grad_att, w_out, ctx, q, k, v, probs, grads, grad_out, gctx):
    half = grad_out.shape[2]
    gctx[...] = dot(grad_att[...], w_out[...], NT).astype(bf16)
    grad = dot(ctx[...], grad_att[...], TN).astype(bf16)
    grad_out[0] = grad[:, :half]
    grad_out[1] = grad[:, half:]
    tokens, width = q.shape
    pairs = width // PAIR
    for t in range(tokens // TILE):
        rows = pl.ds(t * TILE, TILE)
        for p in range(pairs):
            lanes = pl.ds(p * PAIR, PAIR)
            prob = probs[t * pairs + p]
            context = both_heads(gctx[rows, lanes])
            grads[rows, pl.ds(2 * width + p * PAIR, PAIR)] = dot(prob, context, TN).astype(bf16)
            grad_prob = dot(context, v[rows, lanes], NT)
            prob = prob.astype(f32)
            mean = jnp.sum(prob * grad_prob, axis=-1, keepdims=True)
            score = (prob * (grad_prob - mean)).astype(bf16)
            grads[rows, lanes] = (side_by_side(dot(score, k[rows, lanes])) * SCALE).astype(bf16)
            queries = both_heads(q[rows, lanes])
            grads[rows, pl.ds(width + p * PAIR, PAIR)] = (dot(score, queries, TN) * SCALE).astype(bf16)


def qkv_grad(
    me, x_t, own, own_out, oth, oth_out, sums_one, sums_two, ffn_own, ffn_other, away, keep, grads, small,
):
    mx, mc, m0 = me[X], me[C], me[Z0]
    half = keep.shape[5]
    size = half // 8
    small[...] = jnp.zeros_like(small)
    for h, g, out, ffn in ((0, own, own_out, ffn_own), (1, oth, oth_out, ffn_other)):
        grads[h] = dot(x_t[...], g[...]).astype(bf16)
        rows = [s[i : i + 1, j * half : (j + 1) * half] for s in (sums_one, sums_two) for i in range(3) for j in range(2)]
        rows += [ffn[i] for i in range(4)]
        rows += [
            jnp.sum(g[:, c * half : (c + 1) * half].astype(f32), axis=0, keepdims=True) for c in (0, 2)
        ]
        for i, row in enumerate(rows):
            small[h, i // 2, i % 2 : i % 2 + 1] = row
        for core, piece in ((1 - mc, away), (mc, keep)):
            for rx in range(2):
                for r0 in range(2):
                    place = 4 * core + 2 * (mx ^ rx) + (m0 ^ r0)
                    for j in range(2):
                        to = (*slot(core, h, rx, r0), j)
                        for c in range(3):
                            piece[*to, c * size : (c + 1) * size, :] = grads[
                                h, rows_at(size * (2 * place + j), size), c * half : (c + 1) * half
                            ]
                        piece[*to, 3 * size : 4 * size, :] = out[j, rows_at(size * place, size), :]
                        piece[*to, 4 * size : 4 * size + 16, :] = split(small[h, 2 * place + j])


def split(values):
    high = values.astype(bf16).astype(f32)
    rest = values - high
    middle = rest.astype(bf16).astype(f32)
    fill = jnp.zeros((10, values.shape[1]), f32)
    return jnp.concatenate([high, middle, rest - middle, fill], axis=0).astype(bf16)


def joined(rows):
    rows = rows.astype(f32)
    return rows[0:2] + rows[2:4] + rows[4:6]


def token_grad(me, grad_one, own, oth, w_own, w_other, out):
    total = grad_one[...]
    half = w_own.shape[2]
    for g, w in ((own, w_own), (oth, w_other)):
        for c in range(3):
            total += dot(g[:, c * half : (c + 1) * half], w[c], NT)
    out[...] = total.astype(bf16)


def place_rows(by_rows, me, b0, b1, b2, b3, out):
    size, width = b0.shape[2:]
    for place in range(4):
        rx, r0 = me[X] ^ (place // 2), me[Z0] ^ (place % 2)
        for c, blocks in ((0, (b0, b2)), (1, (b1, b3))):
            core = me[C] ^ c
            for last, block in enumerate(blocks):

                @pl.when(jnp.where(core == 0, rx, r0) == last)
                def _():
                    for j in range(2):
                        start = (2 * core + j) * size
                        start = pl.multiple_of(start + place * 4 * size if by_rows else start, 8)
                        lanes = slice(0, width) if by_rows else slice(place * width, (place + 1) * width)
                        out[pl.ds(start, size), lanes] = block[jnp.where(core == 0, r0, rx), j].astype(f32)


def place_attn(me, b0, b1, b2, b3, qkv, w_out, attn_bias, res_bias, ffn_bias, gains, shifts, small):
    half = b0.shape[3]
    size = half // 8
    for c, blocks in ((0, (b0, b2)), (1, (b1, b3))):
        core = me[C] ^ c
        for last, block in enumerate(blocks):
            for inner in range(2):
                rx, r0 = jnp.where(core == 0, last, inner), jnp.where(core == 0, inner, last)
                start = 4 * core + 2 * (me[X] ^ rx) + (me[Z0] ^ r0)
                for j in range(2):
                    rows = pl.ds(pl.multiple_of((2 * start + j) * size, 8), size)
                    for n in range(3):
                        qkv[n, rows, :] = block[inner, j, n * size : (n + 1) * size].astype(f32)
                    rows = pl.ds(pl.multiple_of(start * size, 8), size)
                    w_out[rows, j * half : (j + 1) * half] = block[inner, j, 3 * size : 4 * size].astype(f32)
                    small[2 * start + j] = joined(block[inner, j, 4 * size : 4 * size + 16])
    row = lambda i: small[i // 2, i % 2 : i % 2 + 1]
    for out, first in ((res_bias, 0), (gains, 2), (shifts, 4)):
        for i in range(2):
            for j in range(2):
                out[i : i + 1, j * half : (j + 1) * half] = row(first + 6 * i + j)
    for i in range(4):
        ffn_bias[pl.ds(i * half, half)] = row(12 + i).reshape(half)
    for i in range(2):
        attn_bias[i : i + 1] = row(16 + i)


def add_parts(places, small, me, *refs):
    *ins, out = refs
    lead = out.shape[:-2]
    for i in range(math.prod(lead)):
        at = tuple(int(v) for v in np.unravel_index(i, lead))
        total = ins[0][(*places[0], *at)].astype(f32)
        for place, part in zip(places[1:], ins[1:]):
            total += part[(*place, *at)].astype(f32)
        if small:
            n = out.shape[-2] - 16
            tails = [part[(*place, *at)][n:] for place, part in zip(places, ins)]
            out[(*at, slice(0, n))] = total[:n].astype(out.dtype)
            out[(*at, slice(n, n + 16))] = split(sum(joined(t) for t in tails))
        else:
            out[at] = total.astype(out.dtype)


def join(me, a, b, out):
    out[0] = a[...]
    out[1] = b[...]


def tick(me, x, out):
    out[...] = x[...]


def choose(me, a, b, out):
    @pl.when(me[C] == 0)
    def _():
        out[...] = a[...]

    @pl.when(me[C] == 1)
    def _():
        out[...] = b[...]


def mask_bias(bucket, length_row, side, count):
    width = jnp.where(bucket == 0, 32, jnp.where(bucket == 1, 64, 128)).astype(jnp.int32)
    place = side * count + jnp.arange(count, dtype=jnp.int32)
    slot = place // width
    inside = place - slot * width
    match = slot[:, None] == jnp.arange(length_row.shape[0], dtype=jnp.int32)[None, :]
    length = jnp.sum(jnp.where(match, length_row[None, :], 0), axis=1)
    slot, key_ok = slot.reshape(-1, TILE), (inside < length).reshape(-1, TILE)
    same = slot[:, :, None] == slot[:, None, :]
    return jnp.where(same & key_ok[:, None, :], 0.0, NEG).astype(f32)


ORDER = (
    "back", "in1", "B_S0", "in2", "ab2", "I_S0", "ab1+B_p0", "qkv", "B_S1", "A_S0", "B_S2+I_p0",
    "tok", "I_S1", "B_S3", "A_S1", "I_S2", "A_S2", "B_A0", "I_S3", "A_S3", "I_A0+B_g0", "B_A1",
    "A_A0", "I_A1+B_gc", "A_A1", "B_P+I_gc", "I_P+A_gc", "A_P",
)
def per_device(
    dp_size, tokens, w_qkv, attn_bias, w_out, res_bias, w_in, ffn_bias, w_back,
    norm_gains, norm_shifts, cotangent, buckets, lengths,
):
    here = lax.axis_index("dp")
    side = lax.axis_index("tensor")
    n_bits = dp_size.bit_length() - 1
    assert 1 << n_bits == dp_size and n_bits >= 4

    def bit(b):
        return (here >> b) & 1

    me = jnp.stack([bit(1), bit(0), bit(2), bit(3), side]).astype(jnp.int32)

    def over_dp(value, b):
        return lax.ppermute(value, "dp", [(i, i ^ (1 << b)) for i in range(dp_size)])

    def over_tensor(value):
        return lax.ppermute(value, "tensor", [(0, 1), (1, 0)])

    y, x, z0, z1 = 1, 4, 8, 16
    reduce_steps = (y, z0), (x, y), (z0, x)
    gather_steps = (z0, x), (x, z0)

    def flip(value, partners):
        pairs = [(i, i ^ partners[(i >> 1) & 1]) for i in range(2 * dp_size)]
        return lax.ppermute(value, ("dp", "tensor"), pairs)

    n_tokens, model = tokens.shape
    half = w_qkv.shape[2]
    hidden_half = w_in.shape[1]
    quarter = hidden_half // 4
    n_units = n_tokens // TILE * (half // PAIR)

    def after(value, *others):
        return lax.optimization_barrier((value, *others))[0]

    clock = [me]
    waits = []

    def step(body, *inputs, wait=()):
        flat, tree = jax.tree.flatten(inputs)
        held = lax.optimization_barrier((*flat, clock[0], *jax.tree.leaves(wait), *waits))
        waits.clear()
        out = body(*jax.tree.unflatten(tree, held[: len(flat)]))
        clock[0] = jax.tree.leaves(out)[0]
        return out

    def kernel(body, name, ins, outs, scratch=(), wait=(), cost=COST):
        return step(lambda *a: call(body, name, me, a, outs, scratch=scratch, cost=cost), *ins, wait=wait)

    near_shape = sds((4, model // 8, half))
    feed_shape = sds((model, quarter))
    near, = packed(functools.partial(pack_attn, False), "pack_near", me, (w_qkv, w_out), [near_shape])
    near_y = over_tensor(near)
    clock[0] = near
    biases, = kernel(pack_biases, "pack_biases", (attn_bias, ffn_bias), [sds((6, 1, quarter), f32)])
    biases_other = over_tensor(biases)

    def pack(body, name, opposite, weights, shape, wait=()):
        out, = step(
            lambda *w: packed(functools.partial(body, opposite), name, me, w, [shape]), *weights, wait=wait
        )
        return over_tensor(out)

    feed_y = pack(pack_feed, "pack_feed", False, (w_in, w_back), feed_shape)
    near_z, near_x = over_dp(near_y, 2), over_dp(near_y, 1)
    mask = step(lambda b, l: mask_bias(b, l, side, n_tokens), buckets[0], lengths[0])

    act = sds((n_tokens, half))
    probs = sds((n_units, 2 * TILE, TILE))
    wide = sds((n_tokens, model), f32)
    column = sds((n_tokens, 1), f32)
    own_q, own_k, own_v, own_p, own_ctx, tokens_t = kernel(
        attend_own, "attend_own", (tokens, w_qkv, biases, mask),
        [act, act, act, probs, act, sds((model, n_tokens))], cost=LITTLE,
    )
    near_c = [over_dp(after(v, own_ctx), 0) for v in (near_y, near_z, near_x)]
    passed, = kernel(choose, "choose", (near_z, near_x), [near_shape])
    near_d = flip(passed, (x, z0))
    feed_z, feed_x = over_dp(feed_y, 2), over_dp(feed_y, 1)
    turn, = kernel(tick, "tick", (mask[0, :8],), [sds((8, TILE), f32)], wait=(feed_y, biases_other, *near_c))
    feed_d_y = pack(pack_feed, "pack_feed_d", True, (w_in, w_back), feed_shape)
    near_all = near_y, near_z, near_x, near_d
    near_c.append(over_dp(after(near_d, turn), 0))
    (oth_q, oth_k, oth_v, oth_p, oth_ctx, w_qkv_other, w_out_other, mid, mid_low, n1, r1) = kernel(
        attend_other, "attend_other",
        (tokens, *near_all, *near_c, biases_other, mask, own_ctx, w_out,
         res_bias, norm_gains, norm_shifts),
        [act, act, act, probs, act, sds(w_qkv.shape), sds(w_out.shape), wide, sds(tokens.shape), wide, column],
        cost=LITTLE,
    )

    hidden_own, slope_own, total_own, mid_t = kernel(
        feed_own, "feed_own", (mid_low, w_in, biases, w_back),
        [sds((n_tokens, hidden_half)), sds((n_tokens, hidden_half)), wide, sds((model, n_tokens))],
        wait=feed_y, cost=LITTLE,
    )
    feed_all = feed_y, feed_z, feed_x, feed_d_y
    feed_c = [over_dp(after(feed_y, mid_low), 0)] + [over_dp(after(v, total_own), 0) for v in feed_all[1:]]
    (hidden_other, slope_other, w_in_other, w_back_other, output, grad_two, fed, sums_two) = kernel(
        feed_other, "feed_other",
        (mid_low, biases_other, *feed_all, *feed_c, total_own, mid, cotangent,
         res_bias, norm_gains, norm_shifts),
        [sds((n_tokens, hidden_half)), sds((n_tokens, hidden_half)), sds(w_in.shape),
         sds(w_back.shape), sds(tokens.shape), wide, sds(tokens.shape), sds((3, model), f32)],
    )

    env = {}
    ops = {}
    flying = {}

    def sent(key, value):
        flying[key] = value
        return value

    def chain(name, finish):
        state = {}

        def add(name_of, parts, places, shape):
            body = functools.partial(add_parts, places, name == "A")
            return kernel(body, name_of, parts, [sds(shape)])[0]

        def reduce(i):
            def run():
                if i == 0:
                    state["parts"], state["places"] = list(env[name]), [(), ()]
                parts, places = state["parts"], state["places"]
                value = add("add_half", parts, [(*p, 1) for p in places], parts[0].shape[i + 1 :])
                parts.append(sent(f"{name}_p{i}", flip(value, reduce_steps[i])))
                state["places"] = [(*p, 0) for p in places] + [()]

            return run

        def exchange():
            value = add("add_all", state["parts"], state["places"], state["parts"][-1].shape)
            state["pair"] = value, sent(name + "_p3", flip(value, (z1, z1)))

        def gather(i):
            def run():
                pair = state["pair"]
                if i == 0:
                    value = add("add_two", pair, [(), ()], pair[0].shape)
                    for b in range(4, n_bits):
                        value = add("add_two", (value, over_dp(value, b)), [(), ()], value.shape)
                else:
                    value, = kernel(join, "join", pair, [sds((2, *pair[0].shape))])
                got = sent(f"{name}_g{i}", flip(value, gather_steps[i]))
                state["pair"] = value, got
                if i == 1:
                    value_c = sent(name + "_gc", over_dp(value, 0))
                    state["blocks"] = value, value_c, got
                    if name != "A":
                        core_end()

            return run

        for i in range(3):
            ops[f"{name}_S{i}"] = reduce(i)
        ops[name + "_S3"] = exchange
        for i in range(2):
            ops[f"{name}_A{i}"] = gather(i)

        def core_end():
            got = state["blocks"][2]
            state["blocks"] = *state["blocks"], over_dp(after(got, clock[0]) if name == "A" else got, 0)

        def place():
            if name == "A":
                core_end()
            env[name + "_result"] = finish(state["blocks"])

        ops[name + "_P"] = place

    sub = quarter // 4
    piece = sds((2, 2, 2, 2, sub, model))
    in_piece = sds((2, 2, 2, 2, model // 4, quarter))
    attn_piece = sds((2, 2, 2, 2, half // 2 + 16, half))
    raw_out = sds((2, half, model // 2))

    def back():
        away, keep = kernel(
            back_grad, "back_grad", (hidden_own, hidden_other, fed), [piece, piece],
            scratch=[pltpu.VMEM((2, hidden_half, model), bf16)],
        )
        env["B"] = keep, sent("B_c", over_dp(away, 0))

    def in_first():
        env["in_own"] = kernel(
            in_grad_own, "in_grad_own", (mid_t, fed, w_back, slope_own, w_in),
            [sds(w_in.shape), sds((4, 1, quarter), f32), wide],
        )

    def in_second():
        grads_own, bias_own, mid_own = env["in_own"]
        away, keep, bias_other, grad_one, grad_att, sums_one = kernel(
            in_grad_other, "in_grad_other",
            (mid_t, fed, w_back_other, slope_other, w_in_other, grads_own, mid_own, grad_two, n1, r1, norm_gains),
            [in_piece, in_piece, sds((4, 1, quarter), f32), wide, sds(tokens.shape), sds((3, model), f32)],
            scratch=[pltpu.VMEM(w_in.shape, bf16)],
        )
        env["I"] = keep, sent("I_c", over_dp(away, 0))
        env.update(bias_own=bias_own, bias_other=bias_other, grad_one=grad_one, grad_att=grad_att, sums_one=sums_one)

    def attn_back(w, ctx, q, k, v, p):
        return kernel(
            attend_back, "attend_back", (env["grad_att"], w, ctx, q, k, v, p),
            [sds((n_tokens, 3 * half)), raw_out],
            scratch=[pltpu.VMEM((n_tokens, half), bf16)],
        )

    def attn_first():
        env["own"] = attn_back(w_out, own_ctx, own_q, own_k, own_v, own_p)

    def attn_second():
        env["other"] = attn_back(w_out_other, oth_ctx, oth_q, oth_k, oth_v, oth_p)

    def qkv():
        away, keep = kernel(
            qkv_grad, "qkv_grad",
            (tokens_t, *env["own"], *env["other"], env["sums_one"], sums_two, env["bias_own"], env["bias_other"]),
            [attn_piece, attn_piece],
            scratch=[pltpu.VMEM((2, model, 3 * half), bf16), pltpu.VMEM((2, 16, 2, half), f32)],
        )
        env["A"] = keep, sent("A_c", over_dp(away, 0))

    def token():
        env["grad_tokens"], = kernel(
            token_grad, "token_grad", (env["grad_one"], env["own"][0], env["other"][0], w_qkv, w_qkv_other), [sds(tokens.shape)]
        )

    chain("B", lambda blocks: kernel(
        functools.partial(place_rows, True), "place_back", blocks, [sds(w_back.shape, f32)]
    ))
    chain("I", lambda blocks: kernel(
        functools.partial(place_rows, False), "place_in", blocks, [sds(w_in.shape, f32)]
    ))
    last_shapes = [w_qkv.shape, w_out.shape, (2, half), (2, model), (hidden_half,), (2, model), (2, model)]
    chain("A", lambda blocks: kernel(
        place_attn, "place_attn", blocks, [sds(shape, f32) for shape in last_shapes],
        scratch=[pltpu.VMEM((16, 2, half), f32)],
    ))
    ops.update({
        "back": back, "in1": in_first, "in2": in_second, "ab1": attn_first, "ab2": attn_second,
        "qkv": qkv, "tok": token,
    })
    for entry in ORDER:
        key, *ended = entry.split("+")
        waits.extend(flying.pop(p) for p in ended)
        ops.pop(key)()
    assert not ops
    grad_tokens = env["grad_tokens"]
    (grad_back,), (grad_in,) = env["B_result"], env["I_result"]
    grad_qkv, grad_out, grad_attn_bias, grad_res_bias, grad_ffn_bias, grad_gains, grad_shifts = env["A_result"]

    return (
        output,
        grad_tokens,
        grad_qkv,
        grad_attn_bias,
        grad_out,
        grad_res_bias,
        grad_in,
        grad_ffn_bias,
        grad_back,
        grad_gains,
        grad_shifts,
    )


def solution(mesh):
    dp_size = mesh.shape["dp"]
    placed = (
        P(("dp", "tensor"), None),
        P(None, None, "tensor"),
        P(None, "tensor"),
        P("tensor", None),
        P(),
        P(None, "tensor"),
        P("tensor"),
        P("tensor", None),
        P(),
        P(),
        P(("dp", "tensor"), None),
        P("dp"),
        P("dp", None),
    )
    return jax.shard_map(
        lambda *args: per_device(dp_size, *args),
        mesh=mesh,
        in_specs=placed,
        out_specs=(
            P(("dp", "tensor"), None),
            P(("dp", "tensor"), None),
            P(None, None, "tensor"),
            P(None, "tensor"),
            P("tensor", None),
            P(),
            P(None, "tensor"),
            P("tensor"),
            P("tensor", None),
            P(),
            P(),
        ),
        check_vma=False,
    )
```

```python
import functools
import math

import jax
import jax.numpy as jnp
import numpy as np
from jax import lax
from jax.experimental import pallas as pl
from jax.experimental.pallas import tpu as pltpu
from jax.sharding import PartitionSpec as P

HEAD_DIM = 64
ROW_LEN = 1024
TILE = 128
PAIR = 2 * HEAD_DIM
NEG = -1000000000.0
EPS = 1e-05
SCALE = HEAD_DIM ** (-0.5)
inv_root_two = 1.0 / math.sqrt(2.0)
inv_root_tau = 1.0 / math.sqrt(2.0 * math.pi)
f32 = jnp.float32
bf16 = jnp.bfloat16
MB = 1 << 20
LIMIT = 12
WIDE_LIMIT = 14
WIDE = {"feed_own", "feed_other", "back_grad", "in_grad_own", "in_grad_other", "qkv_grad"}

NN, NT, TN = ((1,), (0,)), ((1,), (1,)), ((0,), (0,))


def dot(a, b, dims=NN):
    return lax.dot_general(a, b, (dims, ((), ())), preferred_element_type=f32)


def sds(shape, dtype=bf16):
    return jax.ShapeDtypeStruct(shape, dtype)


def vmem():
    return pl.BlockSpec(memory_space=pltpu.VMEM)


def smem():
    return pl.BlockSpec(memory_space=pltpu.SMEM)


COST = pl.CostEstimate(flops=3 * 10**10, bytes_accessed=10**15, transcendentals=0)


LITTLE = pl.CostEstimate(flops=1, bytes_accessed=10**15, transcendentals=0)


def call(body, name, me, ins, outs, scratch=(), cost=COST):
    limit = WIDE_LIMIT if name in WIDE else LIMIT
    return pl.pallas_call(
        body,
        name=name,
        out_shape=outs,
        in_specs=[smem()] + [vmem()] * len(ins),
        out_specs=[vmem()] * len(outs),
        scratch_shapes=scratch,
        compiler_params=pltpu.CompilerParams(vmem_limit_bytes=limit * MB),
        cost_estimate=cost,
    )(me, *ins)


def packed(body, name, me, ins, outs, cost=COST):
    return pl.pallas_call(
        body,
        name=name,
        out_shape=outs,
        in_specs=[smem()] + [pl.BlockSpec(memory_space=pltpu.HBM)] * len(ins),
        out_specs=[vmem()] * len(outs),
        scratch_shapes=[pltpu.SemaphoreType.DMA((3,))],
        compiler_params=pltpu.CompilerParams(vmem_limit_bytes=LIMIT * MB),
        cost_estimate=cost,
    )(me, *[pltpu.with_memory_space_constraint(v, pltpu.HBM) for v in ins])


X, C, Z0, Z1, SIDE = range(5)


def rows_at(start, size):
    return pl.ds(pl.multiple_of(start, 16), size)


def head_lanes():
    return lax.broadcasted_iota(jnp.int32, (TILE, PAIR), 1) < HEAD_DIM


def both_heads(block):
    first = head_lanes()
    zero = jnp.zeros_like(block)
    return jnp.concatenate([jnp.where(first, block, zero), jnp.where(first, zero, block)], axis=0)


def side_by_side(stacked):
    return jnp.where(head_lanes(), stacked[:TILE], stacked[TILE:])


def project(x, w, bias, q, k, v):
    q[...] = (dot(x[...], w[0]) + bias[0]).astype(bf16)
    k[...] = dot(x[...], w[1]).astype(bf16)
    v[...] = (dot(x[...], w[2]) + bias[1]).astype(bf16)


def attention(mask, q, k, v, probs, ctx):
    tokens, width = q.shape
    pairs = width // PAIR
    for t in range(tokens // TILE):
        rows = pl.ds(t * TILE, TILE)
        bias = mask[t]
        bias = jnp.concatenate([bias, bias], axis=0)
        for p in range(pairs):
            lanes = pl.ds(p * PAIR, PAIR)
            queries = both_heads(q[rows, lanes] * jnp.asarray(SCALE, bf16))
            scores = dot(queries, k[rows, lanes], NT) + bias
            raised = jnp.exp(scores - jnp.max(scores, axis=-1, keepdims=True))
            prob = (raised / jnp.sum(raised, axis=-1, keepdims=True)).astype(bf16)
            probs[t * pairs + p] = prob
            ctx[rows, lanes] = side_by_side(dot(prob, v[rows, lanes])).astype(bf16)


def attend_own(me, x, w, bias, mask, q, k, v, probs, ctx, x_t):
    x_t[...] = x[...].T
    project(x, w, bias, q, k, v)
    attention(mask, q, k, v, probs, ctx)


def normed(z):
    centred = z - jnp.mean(z, axis=-1, keepdims=True)
    inv = lax.rsqrt(jnp.mean(centred * centred, axis=-1, keepdims=True) + EPS)
    return centred * inv, inv


def norm_back(grad_normed, n, inv):
    return inv * (
        grad_normed
        - jnp.mean(grad_normed, axis=-1, keepdims=True)
        - n * jnp.mean(grad_normed * n, axis=-1, keepdims=True)
    )


def attn_copies(piece, core, w_qkv, w_out, out, sems, first):
    rows = w_qkv.shape[1] // 8
    half = w_qkv.shape[2]
    out_rows = w_out.shape[0] // 8
    mine = w_out.at[rows_at((2 * piece + core) * out_rows, out_rows)]
    pairs = (
        (w_qkv.at[:, rows_at((2 * piece + core) * rows, rows), :], out.at[0:3]),
        (mine.at[:, 0:half], out.at[3, 0:out_rows]),
        (mine.at[:, half : 2 * half], out.at[3, out_rows : 2 * out_rows]),
    )
    return [pltpu.make_async_copy(a, b, sems.at[first + i]) for i, (a, b) in enumerate(pairs)]


def feed_copies(piece, core, w_in, w_back, out, sems, first):
    model, hidden = w_in.shape
    width, rows = hidden // 4, model // 2
    half = width // 2
    mine = w_back.at[rows_at(piece * width + core * half, half)]
    pairs = (
        (w_in.at[rows_at(core * rows, rows), pl.ds(pl.multiple_of(piece * width, 128), width)], out.at[0:rows]),
        (mine.at[:, 0:width], out.at[rows : rows + half]),
        (mine.at[:, width : 2 * width], out.at[rows + half : rows + 2 * half]),
    )
    return [pltpu.make_async_copy(a, b, sems.at[first + i]) for i, (a, b) in enumerate(pairs)]


def run_copies(copies):
    for copy in copies:
        copy.start()
    for copy in copies:
        copy.wait()


def pack_attn(opposite, me, w_qkv, w_out, out, sems):
    piece = 2 * me[X] + me[Z0]
    run_copies(attn_copies(3 - piece if opposite else piece, me[C], w_qkv, w_out, out, sems, 0))


def pack_feed(opposite, me, w_in, w_back, out, sems):
    piece = 2 * me[X] + me[Z0]
    run_copies(feed_copies(3 - piece if opposite else piece, me[C], w_in, w_back, out, sems, 0))


def pack_biases(me, attn_bias, ffn_bias, biases):
    width = biases.shape[2]
    for i in range(2):
        biases[i] = attn_bias[i : i + 1]
    for i in range(4):
        biases[2 + i] = ffn_bias[pl.ds(i * width, width)].reshape(1, width)


def attend_other(
    me, x, n0, n1_, n2, n3, c0, c1, c2, c3, bias, mask, ctx_own, wo_own, res_bias, gains, shifts,
    q, k, v, probs, ctx, w, wo_all, mid, mid_low, n1, r1,
):
    core = me[C]
    rows = n0.shape[1]
    half = wo_all.shape[1] // 2
    part = rows // 2
    for r, (near, across) in enumerate(((n0, c0), (n1_, c1), (n2, c2), (n3, c3))):
        piece = (2 * me[X] + me[Z0]) ^ r
        for c, block in ((core, near), (1 - core, across)):
            w[:, rows_at((2 * piece + c) * rows, rows), :] = block[0:3]
            wo_all[rows_at((2 * piece + c) * part, part), 0:half] = block[3, 0:part]
            wo_all[rows_at((2 * piece + c) * part, part), half : 2 * half] = block[3, part : 2 * part]
    project(x, w, bias, q, k, v)
    attention(mask, q, k, v, probs, ctx)
    attended = dot(ctx_own[...], wo_own[...]) + dot(ctx[...], wo_all[...]) + res_bias[0:1]
    n_one, inv = normed(x[...].astype(f32) + attended)
    n1[...] = n_one
    r1[...] = inv
    value = n_one * gains[0:1] + shifts[0:1]
    mid[...] = value
    mid_low[...] = value.astype(bf16)


def gelu_both(a):
    cdf = 0.5 * (1.0 + lax.erf(a * inv_root_two))
    return a * cdf, cdf + a * jnp.exp(-0.5 * a * a) * inv_root_tau


def feed_own(me, mid_low, w_in, bias, w_back, hidden, slope, total, mid_t):
    row = jnp.concatenate([bias[2 + i] for i in range(4)], axis=1)
    value, grad = gelu_both(dot(mid_low[...], w_in[...]) + row)
    value = value.astype(bf16)
    hidden[...] = value
    slope[...] = grad.astype(bf16)
    total[...] = dot(value, w_back[...])
    mid_t[...] = mid_low[...].T


def feed_other(
    me, mid_low, bias, f0, f1, f2, f3, c0, c1, c2, c3, total, mid, cotangent, res_bias, gains, shifts,
    hidden, slope, w_in, w_back, output, grad_two, fed, sums,
):
    core = me[C]
    model = w_in.shape[0]
    width = w_in.shape[1] // 4
    rows, half = model // 2, width // 2
    for r, (near, across) in enumerate(((f0, c0), (f1, c1), (f2, c2), (f3, c3))):
        for c, block in ((core, near), (1 - core, across)):
            w_in[rows_at(c * rows, rows), r * width : (r + 1) * width] = block[0:rows]
            to = rows_at(r * width + c * half, half)
            w_back[to, 0:width] = block[rows : rows + half]
            w_back[to, width : 2 * width] = block[rows + half : rows + 2 * half]
    row = jnp.concatenate([bias[2 + ((2 * me[X] + me[Z0]) ^ r)] for r in range(4)], axis=1)
    value, grad = gelu_both(dot(mid_low[...], w_in[...]) + row)
    value = value.astype(bf16)
    hidden[...] = value
    slope[...] = grad.astype(bf16)
    ffn = total[...] + res_bias[1:2] + dot(value, w_back[...])
    n2, inv = normed(mid[...] + ffn)
    output[...] = (n2 * gains[1:2] + shifts[1:2]).astype(bf16)
    g = cotangent[...].astype(f32)
    grad = norm_back(g * gains[1:2], n2, inv)
    grad_two[...] = grad
    low = grad.astype(bf16)
    fed[...] = low
    sums[0:1] = jnp.sum(low.astype(f32), axis=0, keepdims=True)
    sums[1:2] = jnp.sum(g * n2, axis=0, keepdims=True)
    sums[2:3] = jnp.sum(g, axis=0, keepdims=True)


def slot(core, own_or_other, rx, r0):
    first = core == 0
    return jnp.where(first, own_or_other, r0), jnp.where(first, rx, own_or_other), jnp.where(first, r0, rx)


def relative(me, h, quarter):
    if h:
        return quarter // 2, quarter % 2
    return me[X] ^ (quarter // 2), me[Z0] ^ (quarter % 2)


def back_grad(me, hid_own, hid_other, fed, away, keep, grads):
    core = me[C]
    width = hid_own.shape[1] // 4
    size = width // 4
    for h, hid in enumerate((hid_own, hid_other)):
        grads[h] = dot(hid[...], fed[...], TN).astype(bf16)
        for q in range(4):
            rx, r0 = relative(me, h, q)
            for c, out in ((1 - core, away), (core, keep)):
                for j in range(2):
                    out[*slot(c, h, rx, r0), j] = grads[h, rows_at(q * width + (2 * c + j) * size, size), :]


def in_grad(mid_t, fed, w_back, slope, w_in, bias_sums, place):
    pre = (dot(fed[...], w_back[...], NT) * slope[...].astype(f32)).astype(bf16)
    width = pre.shape[1] // 4
    sums = jnp.sum(pre.astype(f32), axis=0, keepdims=True)
    for q in range(4):
        bias_sums[place(q)] = sums[:, q * width : (q + 1) * width]
    return dot(mid_t[...], pre).astype(bf16), dot(pre, w_in[...], NT)


def in_grad_own(me, mid_t, fed, w_back, slope, w_in, grads, bias_sums, total):
    grads[...], total[...] = in_grad(mid_t, fed, w_back, slope, w_in, bias_sums, lambda q: q)


def in_grad_other(
    me, mid_t, fed, w_back, slope, w_in, grads_own, total_own, grad_two, n1, r1, gains,
    away, keep, bias_sums, grad_one, grad_att, sums, grads,
):
    core, here = me[C], 2 * me[X] + me[Z0]
    grads[...], part = in_grad(mid_t, fed, w_back, slope, w_in, bias_sums, lambda q: here ^ q)
    width = w_in.shape[1] // 4
    size = w_in.shape[0] // 4
    for h, source in ((0, grads_own), (1, grads)):
        for q in range(4):
            rx, r0 = relative(me, h, q)
            for c, out in ((1 - core, away), (core, keep)):
                for j in range(2):
                    out[*slot(c, h, rx, r0), j] = source[
                        rows_at((2 * c + j) * size, size), q * width : (q + 1) * width
                    ]
    grad_mid = grad_two[...] + total_own[...] + part
    n = n1[...]
    sums[1:2] = jnp.sum(grad_mid * n, axis=0, keepdims=True)
    sums[2:3] = jnp.sum(grad_mid, axis=0, keepdims=True)
    grad = norm_back(grad_mid * gains[0:1], n, r1[...])
    grad_one[...] = grad
    low = grad.astype(bf16)
    grad_att[...] = low
    sums[0:1] = jnp.sum(low.astype(f32), axis=0, keepdims=True)


def attend_back(me, grad_att, w_out, ctx, q, k, v, probs, grads, grad_out, gctx):
    half = grad_out.shape[2]
    gctx[...] = dot(grad_att[...], w_out[...], NT).astype(bf16)
    grad = dot(ctx[...], grad_att[...], TN).astype(bf16)
    grad_out[0] = grad[:, :half]
    grad_out[1] = grad[:, half:]
    tokens, width = q.shape
    pairs = width // PAIR
    for t in range(tokens // TILE):
        rows = pl.ds(t * TILE, TILE)
        for p in range(pairs):
            lanes = pl.ds(p * PAIR, PAIR)
            prob = probs[t * pairs + p]
            context = both_heads(gctx[rows, lanes])
            grads[rows, pl.ds(2 * width + p * PAIR, PAIR)] = dot(prob, context, TN).astype(bf16)
            grad_prob = dot(context, v[rows, lanes], NT)
            prob = prob.astype(f32)
            mean = jnp.sum(prob * grad_prob, axis=-1, keepdims=True)
            score = (prob * (grad_prob - mean)).astype(bf16)
            grads[rows, lanes] = (side_by_side(dot(score, k[rows, lanes])) * SCALE).astype(bf16)
            queries = both_heads(q[rows, lanes])
            grads[rows, pl.ds(width + p * PAIR, PAIR)] = (dot(score, queries, TN) * SCALE).astype(bf16)


def qkv_grad(
    me, x_t, own, own_out, oth, oth_out, sums_one, sums_two, ffn_own, ffn_other, away, keep, grads, small,
):
    mx, mc, m0 = me[X], me[C], me[Z0]
    half = keep.shape[5]
    size = half // 8
    small[...] = jnp.zeros_like(small)
    for h, g, out, ffn in ((0, own, own_out, ffn_own), (1, oth, oth_out, ffn_other)):
        grads[h] = dot(x_t[...], g[...]).astype(bf16)
        rows = [s[i : i + 1, j * half : (j + 1) * half] for s in (sums_one, sums_two) for i in range(3) for j in range(2)]
        rows += [ffn[i] for i in range(4)]
        rows += [
            jnp.sum(g[:, c * half : (c + 1) * half].astype(f32), axis=0, keepdims=True) for c in (0, 2)
        ]
        for i, row in enumerate(rows):
            small[h, i // 2, i % 2 : i % 2 + 1] = row
        for core, piece in ((1 - mc, away), (mc, keep)):
            for rx in range(2):
                for r0 in range(2):
                    place = 4 * core + 2 * (mx ^ rx) + (m0 ^ r0)
                    for j in range(2):
                        to = (*slot(core, h, rx, r0), j)
                        for c in range(3):
                            piece[*to, c * size : (c + 1) * size, :] = grads[
                                h, rows_at(size * (2 * place + j), size), c * half : (c + 1) * half
                            ]
                        piece[*to, 3 * size : 4 * size, :] = out[j, rows_at(size * place, size), :]
                        piece[*to, 4 * size : 4 * size + 16, :] = split(small[h, 2 * place + j])


def split(values):
    high = values.astype(bf16).astype(f32)
    rest = values - high
    middle = rest.astype(bf16).astype(f32)
    fill = jnp.zeros((10, values.shape[1]), f32)
    return jnp.concatenate([high, middle, rest - middle, fill], axis=0).astype(bf16)


def joined(rows):
    rows = rows.astype(f32)
    return rows[0:2] + rows[2:4] + rows[4:6]


def token_grad(me, grad_one, own, oth, w_own, w_other, out):
    total = grad_one[...]
    half = w_own.shape[2]
    for g, w in ((own, w_own), (oth, w_other)):
        for c in range(3):
            total += dot(g[:, c * half : (c + 1) * half], w[c], NT)
    out[...] = total.astype(bf16)


def place_rows(by_rows, me, b0, b1, b2, b3, out):
    size, width = b0.shape[2:]
    for place in range(4):
        rx, r0 = me[X] ^ (place // 2), me[Z0] ^ (place % 2)
        for c, blocks in ((0, (b0, b2)), (1, (b1, b3))):
            core = me[C] ^ c
            for last, block in enumerate(blocks):

                @pl.when(jnp.where(core == 0, rx, r0) == last)
                def _():
                    for j in range(2):
                        start = (2 * core + j) * size
                        start = pl.multiple_of(start + place * 4 * size if by_rows else start, 8)
                        lanes = slice(0, width) if by_rows else slice(place * width, (place + 1) * width)
                        out[pl.ds(start, size), lanes] = block[jnp.where(core == 0, r0, rx), j].astype(f32)


def place_attn(me, b0, b1, b2, b3, qkv, w_out, attn_bias, res_bias, ffn_bias, gains, shifts, small):
    half = b0.shape[3]
    size = half // 8
    for c, blocks in ((0, (b0, b2)), (1, (b1, b3))):
        core = me[C] ^ c
        for last, block in enumerate(blocks):
            for inner in range(2):
                rx, r0 = jnp.where(core == 0, last, inner), jnp.where(core == 0, inner, last)
                start = 4 * core + 2 * (me[X] ^ rx) + (me[Z0] ^ r0)
                for j in range(2):
                    rows = pl.ds(pl.multiple_of((2 * start + j) * size, 8), size)
                    for n in range(3):
                        qkv[n, rows, :] = block[inner, j, n * size : (n + 1) * size].astype(f32)
                    rows = pl.ds(pl.multiple_of(start * size, 8), size)
                    w_out[rows, j * half : (j + 1) * half] = block[inner, j, 3 * size : 4 * size].astype(f32)
                    small[2 * start + j] = joined(block[inner, j, 4 * size : 4 * size + 16])
    row = lambda i: small[i // 2, i % 2 : i % 2 + 1]
    for out, first in ((res_bias, 0), (gains, 2), (shifts, 4)):
        for i in range(2):
            for j in range(2):
                out[i : i + 1, j * half : (j + 1) * half] = row(first + 6 * i + j)
    for i in range(4):
        ffn_bias[pl.ds(i * half, half)] = row(12 + i).reshape(half)
    for i in range(2):
        attn_bias[i : i + 1] = row(16 + i)


def add_parts(places, small, me, *refs):
    *ins, out = refs
    lead = out.shape[:-2]
    for i in range(math.prod(lead)):
        at = tuple(int(v) for v in np.unravel_index(i, lead))
        total = ins[0][(*places[0], *at)].astype(f32)
        for place, part in zip(places[1:], ins[1:]):
            total += part[(*place, *at)].astype(f32)
        if small:
            n = out.shape[-2] - 16
            tails = [part[(*place, *at)][n:] for place, part in zip(places, ins)]
            out[(*at, slice(0, n))] = total[:n].astype(out.dtype)
            out[(*at, slice(n, n + 16))] = split(sum(joined(t) for t in tails))
        else:
            out[at] = total.astype(out.dtype)


def join(me, a, b, out):
    out[0] = a[...]
    out[1] = b[...]


def tick(me, x, out):
    out[...] = x[...]


def choose(me, a, b, out):
    @pl.when(me[C] == 0)
    def _():
        out[...] = a[...]

    @pl.when(me[C] == 1)
    def _():
        out[...] = b[...]


def mask_bias(bucket, length_row, side, count):
    width = jnp.where(bucket == 0, 32, jnp.where(bucket == 1, 64, 128)).astype(jnp.int32)
    place = side * count + jnp.arange(count, dtype=jnp.int32)
    slot = place // width
    inside = place - slot * width
    match = slot[:, None] == jnp.arange(length_row.shape[0], dtype=jnp.int32)[None, :]
    length = jnp.sum(jnp.where(match, length_row[None, :], 0), axis=1)
    slot, key_ok = slot.reshape(-1, TILE), (inside < length).reshape(-1, TILE)
    same = slot[:, :, None] == slot[:, None, :]
    return jnp.where(same & key_ok[:, None, :], 0.0, NEG).astype(f32)


ORDER = (
    "back", "in1", "B_S0", "in2", "ab2", "I_S0", "ab1+B_p0", "qkv", "B_S1", "A_S0", "B_S2+I_p0",
    "tok", "I_S1", "B_S3", "A_S1", "I_S2", "A_S2", "B_A0", "I_S3", "A_S3", "I_A0+B_g0", "B_A1",
    "A_A0", "I_A1+B_gc", "A_A1", "B_P+I_gc", "I_P+A_gc", "A_P",
)
def per_device(
    dp_size, tokens, w_qkv, attn_bias, w_out, res_bias, w_in, ffn_bias, w_back,
    norm_gains, norm_shifts, cotangent, buckets, lengths,
):
    here = lax.axis_index("dp")
    side = lax.axis_index("tensor")
    n_bits = dp_size.bit_length() - 1
    assert 1 << n_bits == dp_size and n_bits >= 4

    def bit(b):
        return (here >> b) & 1

    me = jnp.stack([bit(1), bit(0), bit(2), bit(3), side]).astype(jnp.int32)

    def over_dp(value, b):
        return lax.ppermute(value, "dp", [(i, i ^ (1 << b)) for i in range(dp_size)])

    def over_tensor(value):
        return lax.ppermute(value, "tensor", [(0, 1), (1, 0)])

    y, x, z0, z1 = 1, 4, 8, 16
    reduce_steps = (y, z0), (x, y), (z0, x)
    gather_steps = (z0, x), (x, z0)

    def flip(value, partners):
        pairs = [(i, i ^ partners[(i >> 1) & 1]) for i in range(2 * dp_size)]
        return lax.ppermute(value, ("dp", "tensor"), pairs)

    n_tokens, model = tokens.shape
    half = w_qkv.shape[2]
    hidden_half = w_in.shape[1]
    quarter = hidden_half // 4
    n_units = n_tokens // TILE * (half // PAIR)

    def after(value, *others):
        return lax.optimization_barrier((value, *others))[0]

    clock = [me]
    waits = []

    def step(body, *inputs, wait=()):
        flat, tree = jax.tree.flatten(inputs)
        held = lax.optimization_barrier((*flat, clock[0], *jax.tree.leaves(wait), *waits))
        waits.clear()
        out = body(*jax.tree.unflatten(tree, held[: len(flat)]))
        clock[0] = jax.tree.leaves(out)[0]
        return out

    def kernel(body, name, ins, outs, scratch=(), wait=(), cost=COST):
        return step(lambda *a: call(body, name, me, a, outs, scratch=scratch, cost=cost), *ins, wait=wait)

    near_shape = sds((4, model // 8, half))
    feed_shape = sds((model, quarter))
    near, = packed(functools.partial(pack_attn, False), "pack_near", me, (w_qkv, w_out), [near_shape], LITTLE)
    near_y = over_tensor(near)
    clock[0] = near
    biases, = kernel(pack_biases, "pack_biases", (attn_bias, ffn_bias), [sds((6, 1, quarter), f32)])
    biases_other = over_tensor(biases)

    def pack(body, name, opposite, weights, shape, wait=()):
        out, = step(
            lambda *w: packed(functools.partial(body, opposite), name, me, w, [shape]), *weights, wait=wait
        )
        return over_tensor(out)

    feed_y = pack(pack_feed, "pack_feed", False, (w_in, w_back), feed_shape)
    near_z, near_x = over_dp(near_y, 2), over_dp(near_y, 1)
    mask = step(lambda b, l: mask_bias(b, l, side, n_tokens), buckets[0], lengths[0])

    act = sds((n_tokens, half))
    probs = sds((n_units, 2 * TILE, TILE))
    wide = sds((n_tokens, model), f32)
    column = sds((n_tokens, 1), f32)
    own_q, own_k, own_v, own_p, own_ctx, tokens_t = kernel(
        attend_own, "attend_own", (tokens, w_qkv, biases, mask),
        [act, act, act, probs, act, sds((model, n_tokens))], cost=LITTLE,
    )
    near_c = [over_dp(after(v, own_ctx), 0) for v in (near_y, near_z, near_x)]
    passed, = kernel(choose, "choose", (near_z, near_x), [near_shape])
    near_d = flip(passed, (x, z0))
    feed_z, feed_x = over_dp(feed_y, 2), over_dp(feed_y, 1)
    turn, = kernel(tick, "tick", (mask[0, :8],), [sds((8, TILE), f32)], wait=(feed_y, biases_other, *near_c))
    feed_d_y = pack(pack_feed, "pack_feed_d", True, (w_in, w_back), feed_shape)
    near_all = near_y, near_z, near_x, near_d
    near_c.append(over_dp(after(near_d, turn), 0))
    (oth_q, oth_k, oth_v, oth_p, oth_ctx, w_qkv_other, w_out_other, mid, mid_low, n1, r1) = kernel(
        attend_other, "attend_other",
        (tokens, *near_all, *near_c, biases_other, mask, own_ctx, w_out,
         res_bias, norm_gains, norm_shifts),
        [act, act, act, probs, act, sds(w_qkv.shape), sds(w_out.shape), wide, sds(tokens.shape), wide, column],
        cost=LITTLE,
    )

    hidden_own, slope_own, total_own, mid_t = kernel(
        feed_own, "feed_own", (mid_low, w_in, biases, w_back),
        [sds((n_tokens, hidden_half)), sds((n_tokens, hidden_half)), wide, sds((model, n_tokens))],
        wait=feed_y, cost=LITTLE,
    )
    feed_all = feed_y, feed_z, feed_x, feed_d_y
    feed_c = [over_dp(after(feed_y, mid_low), 0)] + [over_dp(after(v, total_own), 0) for v in feed_all[1:]]
    (hidden_other, slope_other, w_in_other, w_back_other, output, grad_two, fed, sums_two) = kernel(
        feed_other, "feed_other",
        (mid_low, biases_other, *feed_all, *feed_c, total_own, mid, cotangent,
         res_bias, norm_gains, norm_shifts),
        [sds((n_tokens, hidden_half)), sds((n_tokens, hidden_half)), sds(w_in.shape),
         sds(w_back.shape), sds(tokens.shape), wide, sds(tokens.shape), sds((3, model), f32)],
    )

    env = {}
    ops = {}
    flying = {}

    def sent(key, value):
        flying[key] = value
        return value

    def chain(name, finish):
        state = {}

        def add(name_of, parts, places, shape):
            body = functools.partial(add_parts, places, name == "A")
            return kernel(body, name_of, parts, [sds(shape)])[0]

        def reduce(i):
            def run():
                if i == 0:
                    state["parts"], state["places"] = list(env[name]), [(), ()]
                parts, places = state["parts"], state["places"]
                value = add("add_half", parts, [(*p, 1) for p in places], parts[0].shape[i + 1 :])
                parts.append(sent(f"{name}_p{i}", flip(value, reduce_steps[i])))
                state["places"] = [(*p, 0) for p in places] + [()]

            return run

        def exchange():
            value = add("add_all", state["parts"], state["places"], state["parts"][-1].shape)
            state["pair"] = value, sent(name + "_p3", flip(value, (z1, z1)))

        def gather(i):
            def run():
                pair = state["pair"]
                if i == 0:
                    value = add("add_two", pair, [(), ()], pair[0].shape)
                    for b in range(4, n_bits):
                        value = add("add_two", (value, over_dp(value, b)), [(), ()], value.shape)
                else:
                    value, = kernel(join, "join", pair, [sds((2, *pair[0].shape))])
                got = sent(f"{name}_g{i}", flip(value, gather_steps[i]))
                state["pair"] = value, got
                if i == 1:
                    value_c = sent(name + "_gc", over_dp(value, 0))
                    state["blocks"] = value, value_c, got
                    if name != "A":
                        core_end()

            return run

        for i in range(3):
            ops[f"{name}_S{i}"] = reduce(i)
        ops[name + "_S3"] = exchange
        for i in range(2):
            ops[f"{name}_A{i}"] = gather(i)

        def core_end():
            got = state["blocks"][2]
            state["blocks"] = *state["blocks"], over_dp(after(got, clock[0]) if name == "A" else got, 0)

        def place():
            if name == "A":
                core_end()
            env[name + "_result"] = finish(state["blocks"])

        ops[name + "_P"] = place

    sub = quarter // 4
    piece = sds((2, 2, 2, 2, sub, model))
    in_piece = sds((2, 2, 2, 2, model // 4, quarter))
    attn_piece = sds((2, 2, 2, 2, half // 2 + 16, half))
    raw_out = sds((2, half, model // 2))

    def back():
        away, keep = kernel(
            back_grad, "back_grad", (hidden_own, hidden_other, fed), [piece, piece],
            scratch=[pltpu.VMEM((2, hidden_half, model), bf16)],
        )
        env["B"] = keep, sent("B_c", over_dp(away, 0))

    def in_first():
        env["in_own"] = kernel(
            in_grad_own, "in_grad_own", (mid_t, fed, w_back, slope_own, w_in),
            [sds(w_in.shape), sds((4, 1, quarter), f32), wide],
        )

    def in_second():
        grads_own, bias_own, mid_own = env["in_own"]
        away, keep, bias_other, grad_one, grad_att, sums_one = kernel(
            in_grad_other, "in_grad_other",
            (mid_t, fed, w_back_other, slope_other, w_in_other, grads_own, mid_own, grad_two, n1, r1, norm_gains),
            [in_piece, in_piece, sds((4, 1, quarter), f32), wide, sds(tokens.shape), sds((3, model), f32)],
            scratch=[pltpu.VMEM(w_in.shape, bf16)],
        )
        env["I"] = keep, sent("I_c", over_dp(away, 0))
        env.update(bias_own=bias_own, bias_other=bias_other, grad_one=grad_one, grad_att=grad_att, sums_one=sums_one)

    def attn_back(w, ctx, q, k, v, p):
        return kernel(
            attend_back, "attend_back", (env["grad_att"], w, ctx, q, k, v, p),
            [sds((n_tokens, 3 * half)), raw_out],
            scratch=[pltpu.VMEM((n_tokens, half), bf16)],
        )

    def attn_first():
        env["own"] = attn_back(w_out, own_ctx, own_q, own_k, own_v, own_p)

    def attn_second():
        env["other"] = attn_back(w_out_other, oth_ctx, oth_q, oth_k, oth_v, oth_p)

    def qkv():
        away, keep = kernel(
            qkv_grad, "qkv_grad",
            (tokens_t, *env["own"], *env["other"], env["sums_one"], sums_two, env["bias_own"], env["bias_other"]),
            [attn_piece, attn_piece],
            scratch=[pltpu.VMEM((2, model, 3 * half), bf16), pltpu.VMEM((2, 16, 2, half), f32)],
        )
        env["A"] = keep, sent("A_c", over_dp(away, 0))

    def token():
        env["grad_tokens"], = kernel(
            token_grad, "token_grad", (env["grad_one"], env["own"][0], env["other"][0], w_qkv, w_qkv_other), [sds(tokens.shape)]
        )

    chain("B", lambda blocks: kernel(
        functools.partial(place_rows, True), "place_back", blocks, [sds(w_back.shape, f32)]
    ))
    chain("I", lambda blocks: kernel(
        functools.partial(place_rows, False), "place_in", blocks, [sds(w_in.shape, f32)]
    ))
    last_shapes = [w_qkv.shape, w_out.shape, (2, half), (2, model), (hidden_half,), (2, model), (2, model)]
    chain("A", lambda blocks: kernel(
        place_attn, "place_attn", blocks, [sds(shape, f32) for shape in last_shapes],
        scratch=[pltpu.VMEM((16, 2, half), f32)],
    ))
    ops.update({
        "back": back, "in1": in_first, "in2": in_second, "ab1": attn_first, "ab2": attn_second,
        "qkv": qkv, "tok": token,
    })
    for entry in ORDER:
        key, *ended = entry.split("+")
        waits.extend(flying.pop(p) for p in ended)
        ops.pop(key)()
    assert not ops
    grad_tokens = env["grad_tokens"]
    (grad_back,), (grad_in,) = env["B_result"], env["I_result"]
    grad_qkv, grad_out, grad_attn_bias, grad_res_bias, grad_ffn_bias, grad_gains, grad_shifts = env["A_result"]

    return (
        output,
        grad_tokens,
        grad_qkv,
        grad_attn_bias,
        grad_out,
        grad_res_bias,
        grad_in,
        grad_ffn_bias,
        grad_back,
        grad_gains,
        grad_shifts,
    )


def solution(mesh):
    dp_size = mesh.shape["dp"]
    placed = (
        P(("dp", "tensor"), None),
        P(None, None, "tensor"),
        P(None, "tensor"),
        P("tensor", None),
        P(),
        P(None, "tensor"),
        P("tensor"),
        P("tensor", None),
        P(),
        P(),
        P(("dp", "tensor"), None),
        P("dp"),
        P("dp", None),
    )
    return jax.shard_map(
        lambda *args: per_device(dp_size, *args),
        mesh=mesh,
        in_specs=placed,
        out_specs=(
            P(("dp", "tensor"), None),
            P(("dp", "tensor"), None),
            P(None, None, "tensor"),
            P(None, "tensor"),
            P("tensor", None),
            P(),
            P(None, "tensor"),
            P("tensor"),
            P("tensor", None),
            P(),
            P(),
        ),
        check_vma=False,
    )
```
